32 devices in a mesh: req: 8 (over y, x, core), blk: 4 (over z).
Axes of the slice: x: 2, y: 2, z: 4, core: 2. Of those that a mesh axis runs over, the one named last changes fastest.
Arguments:
- x_img: bfloat16 [8, 1024, 1536], P('req', 'blk'), may hold values from -0.3 to 0.3
- x_txt: bfloat16 [8, 154, 1536], P('req'), may hold values from -6 to 6
- modulation: float32 [8, 7, 1536], P('req'), may hold values from -8 to 8
- w_img: bfloat16 [1536, 2304], P(None, 'req'), may hold values from -0.375 to 0.375
- w_txt: bfloat16 [1536, 1536], P(None, 'req'), may hold values from -0.15625 to 0.15625
- w_out: bfloat16 [768, 1536], P('req'), may hold values from -0.21875 to 0.21875
- w_final: bfloat16 [1536, 64], replicated, may hold values from -0.15625 to 0.15625
- lengths: int32 [8], P('req'), may hold values from 16 to 154, as said below
- block_mask: int32 [8, 4, 4], P('req', 'blk'), may hold values from 0 to 1, as said below
- timestep: int32 [8], P('req'), may hold values from 0 to 27
- latent: float32 [8, 16, 32, 128], P('req', None, 'blk'), may hold values from -6 to 6
- conv_w: bfloat16 [512, 144], replicated, may hold values from -0.5 to 0.5
Outputs:
- velocity: float32 [8, 16, 32, 128], P('req', None, 'blk')
- latent_next: float32 [8, 16, 32, 128], P('req', None, 'blk')
- features: bfloat16 [8, 512, 32, 128], P('req', None, 'blk')
The draws below stay inside these ranges and needn't reach their ends.
Inputs may be any that keep to these rules, and one draw needn't show every extreme that they name: Text keys from position lengths[r] on are padding; some request uses all 154 text tokens. Every tile may attend to its own keys: block_mask[r, t, t] = 1.
All inputs are finite; a program needn't handle non-finite values.
Results may differ from the reference program's by a relative error of at most 0.0063.
Values may be sent and summed in bfloat16 or wider, within the bound.
A program may use at most 192 MiB of HBM per device.

```python
import jax
import jax.numpy as jnp
from jax import lax

D = 1536
HD = 64
HEADS = 12
TXT = 154
TOK_DEV = 256
GRIDW = 64
PATCH = 2
LATC = 16
CONVC = 512
NSTEPS = 28
HDIM = 768
REQS = 8
TILES = 4
IMG = 1024
OUTW = 64
LATH = 32
LATW = 128


def draw_x_img(key, part):
    first_key = jax.random.fold_in(key, 0)
    values = 0.04 * jax.random.normal(first_key, (REQS, IMG, D), jnp.float32)
    return jnp.clip(values, -0.3, 0.3).astype(jnp.bfloat16)


def draw_modulation(key, part):
    first_key = jax.random.fold_in(key, 0)
    spread = jnp.array([0.5, 0.3, 1.5, 0.5, 0.3, 0.5, 0.3], jnp.float32)[None, :, None]
    values = spread * jax.random.normal(first_key, (REQS, 7, D), jnp.float32)
    return jnp.clip(values, -8.0, 8.0)


def draw_w_img(key, part):
    first_key, second_key, third_key = jax.random.split(key, 3)
    unit_std = D ** (-0.5)
    query_part = unit_std * jax.random.normal(first_key, (D, HDIM), jnp.float32)
    key_part = unit_std * jax.random.normal(second_key, (D, HDIM), jnp.float32)
    value_part = unit_std * jax.random.normal(third_key, (D, HDIM), jnp.float32)
    values = jnp.concatenate([query_part, key_part, value_part], axis=1)
    return jnp.clip(values, -0.375, 0.375).astype(jnp.bfloat16)


def draw_lengths(key, part):
    first_key, second_key = jax.random.split(key)
    base_rows = jax.random.randint(first_key, (REQS,), TXT // 10 + 1, TXT + 1)
    full_index = jax.random.randint(second_key, (), 0, REQS)
    return jnp.where(jnp.arange(REQS) == full_index, TXT, base_rows).astype(jnp.int32)


def draw_block_mask(key, part):
    first_key, second_key = jax.random.split(key)
    density = jax.random.randint(first_key, (REQS, TILES, 1), 2, 13)
    dice_rolls = jax.random.randint(second_key, (REQS, TILES, TILES), 0, 16)
    diagonal = jnp.arange(TILES)[:, None] == jnp.arange(TILES)[None, :]
    return jnp.where(diagonal[None] | (dice_rolls < density), 1, 0).astype(jnp.int32)


def place_ends(result, key, smallest, high):
    shape = result.shape
    place = [jax.random.randint(jax.random.fold_in(key, axis), (), 0, shape[axis]) for axis in range(len(shape))]
    result = result.at[tuple(place)].set(smallest)
    longest = shape.index(max(shape))
    place[longest] = (place[longest] + 1) % shape[longest]
    return result.at[tuple(place)].set(high)


def levels(key, shape, pieces, least, largest):
    gain = 1.0
    for dim, blocks in pieces:
        draws = jax.random.uniform(jax.random.fold_in(jax.random.fold_in(key, 6), dim), (blocks,), jnp.float32, least / len(pieces), largest / len(pieces))
        gain = gain * jnp.repeat(jnp.exp(draws), shape[dim] // blocks).reshape((-1,) + (1,) * (len(shape) - 1 - dim))
    return gain


def scatter_about(key, extent, deviation, limit, shards=(), held_as=jnp.bfloat16):
    entries = deviation * jax.random.normal(key, extent, jnp.float32)
    if shards:
        entries = entries * levels(key, extent, shards, -0.22, 0.18)
    return jnp.clip(entries, -limit, limit).astype(held_as)


def setup_inputs(seed: int = 0) -> dict:
    streams_of = jax.random.split(jax.random.key(seed), 13)
    x_img = draw_x_img(jax.random.fold_in(streams_of[12], 71), 0)
    x_txt = scatter_about(streams_of[1], (REQS, TXT, D), 1.0, 6.0, ((0, 8),))
    modulation = draw_modulation(jax.random.fold_in(streams_of[12], 71), 0)
    w_img = draw_w_img(jax.random.fold_in(streams_of[12], 71), 0)
    w_txt = scatter_about(streams_of[4], (D, 2 * HDIM), D ** -0.5, 0.15625, ((1, 8),))
    w_out = scatter_about(streams_of[5], (HDIM, D), HDIM ** -0.5, 0.21875, ((0, 8),))
    w_final = scatter_about(streams_of[6], (D, OUTW), D ** -0.5, 0.15625)
    lengths = draw_lengths(jax.random.fold_in(streams_of[12], 71), 0)
    block_mask = draw_block_mask(jax.random.fold_in(streams_of[12], 71), 0)
    timestep = place_ends(jax.random.randint(streams_of[9], (REQS,), 0, NSTEPS), jax.random.fold_in(streams_of[9], 1), 0, NSTEPS - 1).astype(jnp.int32)
    latent = scatter_about(streams_of[10], (REQS, LATC, LATH, LATW), 1.0, 6.0, ((0, 8), (2, 4)), jnp.float32)
    conv_w = scatter_about(streams_of[11], (CONVC, 9 * LATC), (9 * LATC) ** -0.5, 0.5)
    return dict(x_img=x_img, x_txt=x_txt, modulation=modulation, w_img=w_img, w_txt=w_txt, w_out=w_out, w_final=w_final, lengths=lengths, block_mask=block_mask, timestep=timestep, latent=latent, conv_w=conv_w)


NORM_EPS = 1e-06
SHIFT_FACTOR = 3.0
LATENT_SCALE = 1.5305
LATENT_SHIFT = 0.0609
NEG_LARGE = -1e+30
SCORE_SCALE = 0.125

def layer_norm(values):
    values = values.astype(jnp.float32)
    center = values - lax.optimization_barrier(jnp.mean(values, axis=-1, keepdims=True))
    spread = lax.optimization_barrier(jnp.mean(center * center, axis=-1, keepdims=True))
    return center * lax.rsqrt(spread + NORM_EPS)

def modulate(values, shift_row, scale_row):
    return layer_norm(values) * (1.0 + scale_row) + shift_row

def sigma_of(step_index, step_count):
    fraction = 1.0 - step_index.astype(jnp.float32) / step_count
    return SHIFT_FACTOR * fraction / (1.0 + (SHIFT_FACTOR - 1.0) * fraction)

def unpatchify(token_out, grid_width, patch_size, channels):
    patch_rows = token_out.shape[0] // grid_width
    shaped = token_out.reshape(patch_rows, grid_width, patch_size, patch_size, channels)
    shaped = jnp.transpose(shaped, (4, 0, 2, 1, 3))
    return shaped.reshape(channels, patch_rows * patch_size, grid_width * patch_size)

def convolve(padded, conv_w):
    row_count = padded.shape[1] - 2
    col_count = padded.shape[2] - 2
    tap_list = [padded[:, tap_row:tap_row + row_count, tap_col:tap_col + col_count] for tap_row in range(3) for tap_col in range(3)]
    stacked = jnp.stack(tap_list, axis=1).reshape(padded.shape[0] * 9, row_count * col_count)
    convolved = jnp.dot(conv_w, stacked, preferred_element_type=jnp.float32)
    return convolved.reshape(conv_w.shape[0], row_count, col_count)

def attend_request(queries, keys_img, vals_img, keys_txt, vals_txt, length, mask_rows):
    img_count = queries.shape[0]
    txt_count = keys_txt.shape[0]
    tile_of = jnp.arange(img_count, dtype=jnp.int32) // TOK_DEV
    image_allowed = mask_rows[tile_of][:, tile_of] == 1
    text_allowed = jnp.arange(txt_count, dtype=jnp.int32) < length
    allowed = jnp.concatenate([jnp.broadcast_to(text_allowed[None, :], (img_count, txt_count)), image_allowed], axis=1)
    all_keys = jnp.concatenate([keys_txt, keys_img], axis=0)
    all_vals = jnp.concatenate([vals_txt, vals_img], axis=0)

    def one_head(head_index):
        col_start = head_index * HD
        head_q = lax.dynamic_slice_in_dim(queries, col_start, HD, 1)
        head_k = lax.dynamic_slice_in_dim(all_keys, col_start, HD, 1)
        head_v = lax.dynamic_slice_in_dim(all_vals, col_start, HD, 1)
        scores = jnp.dot(head_q, head_k.T, preferred_element_type=jnp.float32) * SCORE_SCALE
        scores = jnp.where(allowed, scores, NEG_LARGE)
        row_max = lax.optimization_barrier(jnp.max(scores, axis=1, keepdims=True))
        weights = jnp.where(allowed, jnp.exp(scores - row_max), 0.0)
        totals = lax.optimization_barrier(jnp.sum(weights, axis=1, keepdims=True))
        summed = jnp.dot(weights.astype(jnp.bfloat16), head_v, preferred_element_type=jnp.float32)
        return summed / totals
    per_head = lax.map(one_head, jnp.arange(HEADS, dtype=jnp.int32))
    return jnp.transpose(per_head, (1, 0, 2)).reshape(img_count, HEADS * HD).astype(jnp.bfloat16)

def reference(x_img, x_txt, modulation, w_img, w_txt, w_out, w_final, lengths, block_mask, timestep, latent, conv_w):

    def one_request(inputs):
        tokens, text_rows, factors, length, mask_rows, step_index, latent_now = inputs
        h_img = modulate(tokens, factors[0], factors[1]).astype(jnp.bfloat16)
        h_txt = modulate(text_rows, factors[3], factors[4]).astype(jnp.bfloat16)
        qkv = jnp.dot(h_img, w_img, preferred_element_type=jnp.float32).astype(jnp.bfloat16)
        kv_txt = jnp.dot(h_txt, w_txt, preferred_element_type=jnp.float32).astype(jnp.bfloat16)
        attended = attend_request(qkv[:, :HDIM], qkv[:, HDIM:2 * HDIM], qkv[:, 2 * HDIM:], kv_txt[:, :HDIM], kv_txt[:, HDIM:], length, mask_rows)
        residual = tokens.astype(jnp.float32) + factors[2] * jnp.dot(attended, w_out, preferred_element_type=jnp.float32)
        final_in = modulate(residual, factors[5], factors[6]).astype(jnp.bfloat16)
        token_out = jnp.dot(final_in, w_final, preferred_element_type=jnp.float32)
        velocity = unpatchify(token_out, GRIDW, PATCH, LATC)
        sigma_step = sigma_of(step_index + 1, NSTEPS) - sigma_of(step_index, NSTEPS)
        latent_next = latent_now + sigma_step * velocity
        decoded = (latent_next / LATENT_SCALE + LATENT_SHIFT).astype(jnp.bfloat16)
        padded = jnp.pad(decoded, ((0, 0), (1, 1), (1, 1)))
        features = convolve(padded, conv_w).astype(jnp.bfloat16)
        return (velocity, latent_next, features)
    velocity, latent_next, features = lax.map(one_request, (x_img, x_txt, modulation, lengths, block_mask, timestep, latent))
    return (velocity, latent_next, features)
```

```python
import jax
import jax.numpy as jnp
from jax import lax
from jax.experimental import pallas as pl
from jax.experimental.pallas import tpu as pltpu
from jax.sharding import PartitionSpec as P

HD = 64
GRIDW = 64
PATCH = 2
LATC = 16
NSTEPS = 28


NORM_EPS = 1e-06
SHIFT_FACTOR = 3.0
LATENT_SCALE = 1.5305
LATENT_SHIFT = 0.0609
NEG_LARGE = -1e30
SCORE_SCALE = 0.125


def with_halo(block, sides, width):
    for axis, dim in sides:
        count = lax.axis_size(axis)
        forward = [(i, i + 1) for i in range(count - 1)]
        backward = [(target, source) for source, target in forward]
        low = lax.ppermute(
            lax.slice_in_dim(block, block.shape[dim] - width, None, axis=dim), axis, forward
        )
        high = lax.ppermute(lax.slice_in_dim(block, 0, width, axis=dim), axis, backward)
        block = jnp.concatenate([low, block, high], axis=dim)
    return block


def layer_norm(values):
    values = values.astype(jnp.float32)
    center = values - jnp.mean(values, axis=-1, keepdims=True)
    spread = jnp.mean(center * center, axis=-1, keepdims=True)
    return center * lax.rsqrt(spread + NORM_EPS)


def modulate(values, shift_row, scale_row):
    return layer_norm(values) * (1.0 + scale_row) + shift_row


def sigma_of(step_index, step_count):
    fraction = 1.0 - step_index.astype(jnp.float32) / step_count
    return SHIFT_FACTOR * fraction / (1.0 + (SHIFT_FACTOR - 1.0) * fraction)


def unpatchify(token_out, grid_width, patch_size, channels):
    patch_rows = token_out.shape[0] // grid_width
    shaped = token_out.reshape(patch_rows, grid_width, patch_size, patch_size, channels)
    shaped = jnp.transpose(shaped, (4, 0, 2, 1, 3))
    return shaped.reshape(channels, patch_rows * patch_size, grid_width * patch_size)


def convolve(padded, conv_w):
    row_count = padded.shape[1] - 2
    col_count = padded.shape[2] - 2
    tap_list = [
        padded[:, tap_row : tap_row + row_count, tap_col : tap_col + col_count]
        for tap_row in range(3)
        for tap_col in range(3)
    ]
    stacked = jnp.stack(tap_list, axis=1).reshape(padded.shape[0] * 9, row_count * col_count)
    convolved = jnp.dot(conv_w, stacked, preferred_element_type=jnp.float32)
    return convolved.reshape(conv_w.shape[0], row_count, col_count)


def text_state(queries, keys_txt, vals_txt, length):
    text_allowed = (jnp.arange(keys_txt.shape[0], dtype=jnp.int32) < length)[None, None, :]
    text_scores = (
        jnp.einsum("qhd,khd->qhk", queries, keys_txt, preferred_element_type=jnp.float32)
        * SCORE_SCALE
    )
    text_scores = jnp.where(text_allowed, text_scores, NEG_LARGE)
    text_max = jnp.max(text_scores, axis=2)
    text_weights = jnp.where(text_allowed, jnp.exp(text_scores - text_max[:, :, None]), 0.0)
    text_acc = jnp.einsum(
        "qhk,khd->qhd",
        text_weights.astype(jnp.bfloat16),
        vals_txt,
        preferred_element_type=jnp.float32,
    )
    return (text_max, jnp.sum(text_weights, axis=2), text_acc)


def absorb_block(previous, queries, head_keys, head_vals, allowed):
    old_max, old_sum, old_acc = previous
    scores = (
        jnp.einsum("qhd,khd->qhk", queries, head_keys, preferred_element_type=jnp.float32)
        * SCORE_SCALE
    )
    scores = jnp.where(allowed, scores, NEG_LARGE)
    new_max = jnp.maximum(old_max, jnp.max(scores, axis=2))
    weights = jnp.where(allowed, jnp.exp(scores - new_max[:, :, None]), 0.0)
    factor = jnp.exp(old_max - new_max)
    summed = jnp.einsum(
        "qhk,khd->qhd", weights.astype(jnp.bfloat16), head_vals, preferred_element_type=jnp.float32
    )
    return (
        new_max,
        old_sum * factor + jnp.sum(weights, axis=2),
        old_acc * factor[:, :, None] + summed,
    )


def absorb_maybe(previous, queries, head_keys, head_vals, allowed):
    return absorb_block(previous, queries, head_keys, head_vals, allowed)


def on_device(
    x_img,
    x_txt,
    modulation,
    w_img,
    w_txt,
    w_out,
    w_final,
    lengths,
    block_mask,
    timestep,
    latent,
    conv_w,
):
    tokens = x_img[0]
    factors = modulation[0]
    tok_rows = tokens.shape[0]
    head_cols = w_out.shape[0] * lax.axis_size("req")
    head_count = head_cols // HD
    h_img = modulate(tokens, factors[0], factors[1]).astype(jnp.bfloat16)
    h_txt = modulate(x_txt[0], factors[3], factors[4]).astype(jnp.bfloat16)
    qkv = jnp.dot(
        h_img, lax.all_gather(w_img, "req", axis=1, tiled=True), preferred_element_type=jnp.float32
    ).astype(jnp.bfloat16)
    kv_txt = jnp.dot(
        h_txt, lax.all_gather(w_txt, "req", axis=1, tiled=True), preferred_element_type=jnp.float32
    ).astype(jnp.bfloat16)
    keys_txt = kv_txt[:, :head_cols].reshape(-1, head_count, HD)
    vals_txt = kv_txt[:, head_cols:].reshape(-1, head_count, HD)
    length = lengths[0]
    queries = qkv[:, :head_cols].reshape(tok_rows, head_count, HD)
    keys_img = qkv[:, head_cols : 2 * head_cols]
    vals_img = qkv[:, 2 * head_cols :]
    mask_row = block_mask[0, 0]
    tile_count = mask_row.shape[0]
    start_state = text_state(queries, keys_txt, vals_txt, length)
    piece_keys = lax.all_gather(keys_img, "blk", axis=0, tiled=True)
    piece_vals = lax.all_gather(vals_img, "blk", axis=0, tiled=True)
    piece_len = piece_keys.shape[0]
    key_tile = jnp.arange(piece_len, dtype=jnp.int32) // tok_rows
    tile_hit = key_tile[:, None] == jnp.arange(tile_count, dtype=jnp.int32)[None, :]
    allowed = jnp.sum(jnp.where(tile_hit, mask_row[None, :], 0), axis=1) == 1
    head_keys = piece_keys.reshape(piece_len, head_count, HD)
    head_vals = piece_vals.reshape(piece_len, head_count, HD)
    run_max, run_sum, run_acc = absorb_maybe(
        start_state, queries, head_keys, head_vals, allowed[None, None, :]
    )
    attended = (run_acc / run_sum[:, :, None]).reshape(tok_rows, head_cols).astype(jnp.bfloat16)
    projected = jnp.dot(
        attended,
        lax.all_gather(w_out, "req", axis=0, tiled=True),
        preferred_element_type=jnp.float32,
    )
    residual = tokens.astype(jnp.float32) + factors[2] * projected
    final_in = modulate(residual, factors[5], factors[6]).astype(jnp.bfloat16)
    token_out = jnp.dot(final_in, w_final, preferred_element_type=jnp.float32)
    velocity = unpatchify(token_out, GRIDW, PATCH, LATC)[None]
    step_index = timestep[0]
    sigma_step = sigma_of(step_index + 1, NSTEPS) - sigma_of(step_index, NSTEPS)
    latent_next = latent + sigma_step * velocity
    decoded = (latent_next / LATENT_SCALE + LATENT_SHIFT).astype(jnp.bfloat16)
    padded = with_halo(decoded, (("blk", 2),), 1)
    padded = jnp.pad(padded[0], ((0, 0), (0, 0), (1, 1)))
    features = convolve(padded, conv_w).astype(jnp.bfloat16)[None]
    return (velocity, latent_next, features)


MESH = pl.DeviceIdType.MESH
NTILE = 4
NREQ = 8
CHUNK = 96
TXT_PAD = 256
F32 = jnp.float32
BF16 = jnp.bfloat16


def nt_dot(a, b):
    return lax.dot_general(a, b, (((1,), (1,)), ((), ())), preferred_element_type=F32)


def flip(r, bit):
    return r + bit - 2 * bit * ((r // bit) % 2)


def normed(v):
    v = v.astype(F32)
    c = v - jnp.mean(v, axis=-1, keepdims=True)
    return c * lax.rsqrt(jnp.mean(c * c, axis=-1, keepdims=True) + NORM_EPS)


def kernel(
    x_ref, xt_ref, mod_ref, wi_ref, wt_ref, wo_ref, wf_ref, bias_ref, ss_ref, lat_ref,
    vel_ref, next_ref, stk_ref,
    H, HT, WI, WT, WO, Q, K, V, BIAS, A, AT, FIN, DEC,
    z_send, h_recv, b_send, b_recv, wi_send, wi_recv, wt_send, wt_recv,
    wo_send, wo_recv, a_send, a_recv, d_send, d_recv, l_sem,
):
    r = lax.axis_index("req")
    z = lax.axis_index("blk")
    rows = x_ref.shape[0]
    tokens = rows * NTILE
    group = WI.shape[0] // 3
    sib = flip(r, 1)
    nx = flip(r, 2)
    ny = flip(r, 4)
    nd = flip(nx, 4)

    def rcopy(src, dst, ss, rs, **dev):
        return pltpu.make_async_remote_copy(
            src_ref=src, dst_ref=dst, send_sem=ss, recv_sem=rs, device_id=dev, device_id_type=MESH
        )

    barrier = pltpu.get_barrier_semaphore()
    for step in range(1, NREQ):
        pl.semaphore_signal(
            barrier, inc=1, device_id={"req": lax.rem(r + step, NREQ)}, device_id_type=MESH
        )
    for step in range(1, NTILE):
        pl.semaphore_signal(
            barrier, inc=1, device_id={"blk": lax.rem(z + step, NTILE)}, device_id_type=MESH
        )
    pl.semaphore_wait(barrier, NREQ - 1 + NTILE - 1)

    pieces = []
    for j in range(6):
        cid = 8 * (j // 2) + 2 * z + j % 2
        off = pl.multiple_of((cid % 3) * CHUNK, CHUNK)
        pieces.append(
            (wi_ref.at[pl.ds(off, CHUNK)], WI.at[pl.ds(j * CHUNK, CHUNK)], cid // 3, wi_send.at[j], wi_recv.at[j], l_sem.at[j])
        )
    for j in range(2):
        pieces.append(
            (wt_ref, WT.at[pl.ds(j * group, group)], 4 * j + z, wt_send.at[j], wt_recv.at[j], l_sem.at[6 + j])
        )

    for src, slot, owner, ss, rs, ls in pieces:
        @pl.when(owner == r)
        def _():
            for n, dev in enumerate((nx, ny, nd, sib)):
                rcopy(src, slot, ss.at[n], rs, req=dev).start()
            pltpu.make_async_copy(src, slot, ls).start()

    def norm_rows(i, src, dst, shift, scale):
        at = pl.ds(pl.multiple_of(i * 32, 32), 32)
        dst[at, :] = (normed(src[at, :]) * (1.0 + mod_ref[scale : scale + 1, :]) + mod_ref[shift : shift + 1, :]).astype(BF16)

    own = H.at[z]
    pl.loop(0, rows // 32)(lambda i: norm_rows(i, x_ref, own, 0, 1))

    def up(t):
        return rcopy(H.at[t], H.at[t], z_send.at[0, t], h_recv.at[t], blk=z + 1)

    def down(t):
        return rcopy(H.at[t], H.at[t], z_send.at[1, t], h_recv.at[t], blk=z - 1)

    @pl.when(z < NTILE - 1)
    def _():
        up(z).start()

    @pl.when(z > 0)
    def _():
        down(z).start()

    BIAS[z] = bias_ref[...]
    for step in range(1, NTILE):
        rcopy(BIAS.at[z], BIAS.at[z], b_send.at[step], b_recv.at[NTILE - step], blk=lax.rem(z + step, NTILE)).start()

    pl.loop(0, TXT_PAD // 32)(lambda i: norm_rows(i, xt_ref, HT, 3, 4))

    for src, slot, owner, ss, rs, ls in pieces:
        @pl.when(owner == r)
        def _():
            pltpu.make_async_copy(src, slot, ls).wait()

        @pl.when(owner != r)
        def _():
            rcopy(src, slot, ss.at[0], rs, req=sib).wait_recv()

        far = jnp.logical_and(owner // 2 != r // 2, owner % 2 == r % 2)

        @pl.when(far)
        def _():
            rcopy(slot, slot, ss.at[0], rs, req=sib).start()

    def wo_rows(dev):
        return WO.at[pl.ds(pl.multiple_of(dev * CHUNK, CHUNK), CHUNK)]

    for n, (k, dev) in enumerate(((2, nx), (4, ny), (6, nd), (1, sib))):
        rcopy(wo_ref, wo_rows(r), wo_send.at[n], wo_recv.at[k], req=dev).start()
    pltpu.make_async_copy(wo_ref, wo_rows(r), l_sem.at[8]).start()

    kv = nt_dot(HT[...], WT[...]).astype(BF16)
    K[tokens:, :] = kv[:, :group]
    V[tokens:, :] = kv[:, group:]

    def project(t):
        at = pl.ds(pl.multiple_of(t * rows, rows), rows)
        qkv = nt_dot(H[t], WI[...]).astype(BF16)
        Q[at, :] = qkv[:, :group] * jnp.asarray(SCORE_SCALE, BF16)
        K[at, :] = qkv[:, group : 2 * group]
        V[at, :] = qkv[:, 2 * group :]

    project(z)
    for step in range(1, NTILE):
        low, high = z - step, z + step

        @pl.when(low >= 0)
        def _():
            rcopy(H.at[low], H.at[low], z_send.at[0, low], h_recv.at[low], blk=z).wait_recv()

            @pl.when(z < NTILE - 1)
            def _():
                up(low).start()

        @pl.when(high < NTILE)
        def _():
            rcopy(H.at[high], H.at[high], z_send.at[1, high], h_recv.at[high], blk=z).wait_recv()

            @pl.when(z > 0)
            def _():
                down(high).start()

        if step == 1:
            for n, (k, dev) in enumerate(((2, nx), (4, ny), (6, nd))):
                rows_of = wo_rows(dev)
                rcopy(wo_ref, rows_of, wo_send.at[n], wo_recv.at[k], req=sib).wait_recv()
                rcopy(rows_of, rows_of, wo_send.at[4 + n], wo_recv.at[k + 1], req=sib).start()

        @pl.when(low >= 0)
        def _():
            project(low)

        @pl.when(high < NTILE)
        def _():
            project(high)

    for step in range(1, NTILE):
        src = BIAS.at[lax.rem(z + step, NTILE)]
        rcopy(src, src, b_send.at[step], b_recv.at[step], blk=lax.rem(z + step, NTILE)).wait_recv()

    def attend(t):
        at = pl.ds(pl.multiple_of(t * rows, rows), rows)
        bias = BIAS[t][0:1, :]
        q, k, v = Q[at, :], K[...], V[...]
        outs = []
        for h in range(group // HD):
            cols = slice(h * HD, (h + 1) * HD)
            s = nt_dot(q[:, cols], k[:, cols]) + bias
            p = jnp.exp(s - jnp.max(s, axis=1, keepdims=True))
            total = jnp.sum(p, axis=1, keepdims=True)
            o = jnp.dot(p.astype(BF16), v[:, cols], preferred_element_type=F32)
            outs.append(o / total)
        return jnp.concatenate(outs, axis=1).astype(BF16)

    for step in range(1, NTILE):
        t = lax.rem(z + step, NTILE)
        A[step] = attend(t)
        rcopy(A.at[step], AT.at[z], a_send.at[step], a_recv.at[NTILE - step], blk=t).start()
    AT[z] = attend(z)

    pltpu.make_async_copy(wo_ref, wo_rows(r), l_sem.at[8]).wait()
    rcopy(wo_ref, wo_rows(sib), wo_send.at[3], wo_recv.at[1], req=sib).wait_recv()
    for n, (k, dev) in enumerate(((3, nx), (5, ny), (7, nd))):
        rcopy(wo_ref, wo_rows(flip(dev, 1)), wo_send.at[4 + n], wo_recv.at[k], req=sib).wait_recv()
    for step in range(1, NTILE):
        src = AT.at[lax.rem(z + step, NTILE)]
        rcopy(src, src, a_send.at[step], a_recv.at[step], blk=lax.rem(z + step, NTILE)).wait_recv()

    def out_rows(i):
        at = pl.ds(pl.multiple_of(i * 64, 64), 64)
        proj = jnp.dot(AT[0, at, :], WO[0:group, :], preferred_element_type=F32)
        for s in range(1, NTILE):
            proj += jnp.dot(AT[s, at, :], WO[s * group : (s + 1) * group, :], preferred_element_type=F32)
        res = x_ref[at, :].astype(F32) + mod_ref[2:3, :] * proj
        FIN[at, :] = (normed(res) * (1.0 + mod_ref[6:7, :]) + mod_ref[5:6, :]).astype(BF16)

    pl.loop(0, rows // 64)(out_rows)

    dup = (
        lax.broadcasted_iota(jnp.int32, (2 * rows, rows), 0) // 2
        == lax.broadcasted_iota(jnp.int32, (2 * rows, rows), 1)
    ).astype(F32).astype(BF16)
    twice = jnp.dot(dup, FIN[...], preferred_element_type=F32).astype(BF16)
    tok = jnp.dot(twice, wf_ref[...], preferred_element_type=F32).T
    even = lax.broadcasted_iota(jnp.int32, (LATC, 2 * rows), 1) % 2 == 0
    width = PATCH * GRIDW
    sig = ss_ref[0:1, :]
    for p in range(PATCH):
        base = p * 2 * LATC
        val = jnp.where(even, tok[base : base + LATC], tok[base + LATC : base + 2 * LATC])
        for a in range(rows // GRIDW):
            y = PATCH * a + p
            piece = val[:, a * width : (a + 1) * width]
            nxt = lat_ref[:, y, :] + sig * piece
            vel_ref[:, y, :] = piece
            next_ref[:, y, :] = nxt
            DEC[y + 1] = (nxt / LATENT_SCALE + LATENT_SHIFT).astype(BF16)

    count = PATCH * rows // GRIDW
    go_up = rcopy(DEC.at[count], DEC.at[0], d_send.at[0], d_recv.at[0], blk=z + 1)
    go_down = rcopy(DEC.at[1], DEC.at[count + 1], d_send.at[1], d_recv.at[1], blk=z - 1)

    @pl.when(z < NTILE - 1)
    def _():
        go_up.start()

    @pl.when(z > 0)
    def _():
        go_down.start()

    @pl.when(z == 0)
    def _():
        DEC[0] = jnp.zeros((LATC, width), BF16)

    @pl.when(z == NTILE - 1)
    def _():
        DEC[count + 1] = jnp.zeros((LATC, width), BF16)

    for src, slot, owner, ss, rs, ls in pieces:
        @pl.when(owner == r)
        def _():
            for n, dev in enumerate((nx, ny, nd, sib)):
                rcopy(src, slot, ss.at[n], rs, req=dev).wait_send()

        far = jnp.logical_and(owner // 2 != r // 2, owner % 2 == r % 2)

        @pl.when(far)
        def _():
            rcopy(slot, slot, ss.at[0], rs, req=sib).wait_send()

    for n in range(7):
        rcopy(wo_ref, wo_rows(r), wo_send.at[n], wo_recv.at[1], req=sib).wait_send()
    for t in range(NTILE):
        @pl.when(jnp.logical_and(z < NTILE - 1, t <= z))
        def _():
            up(t).wait_send()

        @pl.when(jnp.logical_and(z > 0, t >= z))
        def _():
            down(t).wait_send()
    for step in range(1, NTILE):
        there = lax.rem(z + step, NTILE)
        rcopy(BIAS.at[z], BIAS.at[z], b_send.at[step], b_recv.at[step], blk=there).wait_send()
        rcopy(A.at[step], AT.at[z], a_send.at[step], a_recv.at[step], blk=there).wait_send()

    @pl.when(z < NTILE - 1)
    def _():
        go_up.wait_send()
        go_down.wait_recv()

    @pl.when(z > 0)
    def _():
        go_down.wait_send()
        go_up.wait_recv()

    lane = lax.broadcasted_iota(jnp.int32, (LATC, width), 1)
    for yy in range(count + 2):
        mid = DEC[yy].astype(F32)
        shifted = (
            jnp.where(lane == 0, 0.0, pltpu.roll(mid, 1, 1)),
            mid,
            jnp.where(lane == width - 1, 0.0, pltpu.roll(mid, width - 1, 1)),
        )
        for a in range(3):
            y = yy - a
            if 0 <= y < count:
                for b in range(3):
                    at = (3 * a + b) * LATC
                    stk_ref[at : at + LATC, y * width : (y + 1) * width] = shifted[b].astype(BF16)


def split_heads(
    x_img, x_txt, modulation, w_img, w_txt, w_out, w_final, lengths, block_mask, timestep, latent, conv_w
):
    rows, model = x_img.shape[1], x_img.shape[2]
    group = w_out.shape[0] * NREQ // NTILE
    tokens = rows * NTILE
    allowed = jnp.concatenate(
        [jnp.repeat(block_mask[0, 0] == 1, rows), jnp.arange(TXT_PAD, dtype=jnp.int32) < lengths[0]]
    )
    bias = jnp.broadcast_to(jnp.where(allowed, 0.0, NEG_LARGE).astype(F32)[None, :], (8, tokens + TXT_PAD))
    step_index = timestep[0]
    sigma_step = sigma_of(step_index + 1, NSTEPS) - sigma_of(step_index, NSTEPS)
    height, width = latent.shape[2], latent.shape[3]
    xt = jnp.pad(x_txt[0], ((0, TXT_PAD - x_txt.shape[1]), (0, 0)))
    vmem = pl.BlockSpec(memory_space=pltpu.VMEM)
    hbm = pl.BlockSpec(memory_space=pl.ANY)
    dma = pltpu.SemaphoreType.DMA
    velocity, latent_next, stacked = pl.pallas_call(
        kernel,
        out_shape=(
            jax.ShapeDtypeStruct((LATC, height, width), F32),
            jax.ShapeDtypeStruct((LATC, height, width), F32),
            jax.ShapeDtypeStruct((9 * LATC, height * width), BF16),
        ),
        in_specs=[vmem, vmem, vmem, hbm, hbm, hbm, vmem, vmem, vmem, vmem],
        out_specs=(vmem, vmem, vmem),
        scratch_shapes=[
            pltpu.VMEM((NTILE, rows, model), BF16),
            pltpu.VMEM((TXT_PAD, model), BF16),
            pltpu.VMEM((3 * group, model), BF16),
            pltpu.VMEM((2 * group, model), BF16),
            pltpu.VMEM((NTILE * group, model), BF16),
            pltpu.VMEM((tokens, group), BF16),
            pltpu.VMEM((tokens + TXT_PAD, group), BF16),
            pltpu.VMEM((tokens + TXT_PAD, group), BF16),
            pltpu.VMEM((NTILE, 8, tokens + TXT_PAD), F32),
            pltpu.VMEM((NTILE, rows, group), BF16),
            pltpu.VMEM((NTILE, rows, group), BF16),
            pltpu.VMEM((rows, model), BF16),
            pltpu.VMEM((height + 2, LATC, width), BF16),
            dma((2, NTILE)),
            dma((NTILE,)),
            dma((NTILE,)),
            dma((NTILE,)),
            dma((6, 4)),
            dma((6,)),
            dma((2, 4)),
            dma((2,)),
            dma((7,)),
            dma((8,)),
            dma((NTILE,)),
            dma((NTILE,)),
            dma((2,)),
            dma((2,)),
            dma((9,)),
        ],
        compiler_params=pltpu.CompilerParams(
            collective_id=0, has_side_effects=True, vmem_limit_bytes=48 * 1024 * 1024
        ),
        name="split_heads",
    )(
        x_img[0], xt, modulation[0], w_img.T, w_txt.T, w_out, w_final, bias,
        jnp.full((8, width), sigma_step, F32), latent[0],
    )
    taps = conv_w.reshape(-1, LATC, 9).transpose(0, 2, 1).reshape(-1, 9 * LATC)
    features = jnp.dot(taps, stacked, preferred_element_type=F32).astype(BF16)
    return velocity[None], latent_next[None], features.reshape(1, -1, height, width)


def solution(mesh):
    fits = mesh.shape["blk"] == NTILE and mesh.shape["req"] == NREQ
    return jax.shard_map(
        split_heads if fits else on_device,
        mesh=mesh,
        in_specs=(
            P("req", "blk", None),
            P("req", None, None),
            P("req", None, None),
            P(None, "req"),
            P(None, "req"),
            P("req", None),
            P(),
            P("req"),
            P("req", "blk", None),
            P("req"),
            P("req", None, "blk", None),
            P(),
        ),
        out_specs=(
            P("req", None, "blk", None),
            P("req", None, "blk", None),
            P("req", None, "blk", None),
        ),
        check_vma=False,
    )
```

```python
import jax
import jax.numpy as jnp
from jax import lax
from jax.experimental import pallas as pl
from jax.experimental.pallas import tpu as pltpu
from jax.sharding import PartitionSpec as P

HD = 64
GRIDW = 64
PATCH = 2
LATC = 16
NSTEPS = 28


NORM_EPS = 1e-06
SHIFT_FACTOR = 3.0
LATENT_SCALE = 1.5305
LATENT_SHIFT = 0.0609
NEG_LARGE = -1e30
SCORE_SCALE = 0.125


def with_halo(block, sides, width):
    for axis, dim in sides:
        count = lax.axis_size(axis)
        forward = [(i, i + 1) for i in range(count - 1)]
        backward = [(target, source) for source, target in forward]
        low = lax.ppermute(
            lax.slice_in_dim(block, block.shape[dim] - width, None, axis=dim), axis, forward
        )
        high = lax.ppermute(lax.slice_in_dim(block, 0, width, axis=dim), axis, backward)
        block = jnp.concatenate([low, block, high], axis=dim)
    return block


def layer_norm(values):
    values = values.astype(jnp.float32)
    center = values - jnp.mean(values, axis=-1, keepdims=True)
    spread = jnp.mean(center * center, axis=-1, keepdims=True)
    return center * lax.rsqrt(spread + NORM_EPS)


def modulate(values, shift_row, scale_row):
    return layer_norm(values) * (1.0 + scale_row) + shift_row


def sigma_of(step_index, step_count):
    fraction = 1.0 - step_index.astype(jnp.float32) / step_count
    return SHIFT_FACTOR * fraction / (1.0 + (SHIFT_FACTOR - 1.0) * fraction)


def unpatchify(token_out, grid_width, patch_size, channels):
    patch_rows = token_out.shape[0] // grid_width
    shaped = token_out.reshape(patch_rows, grid_width, patch_size, patch_size, channels)
    shaped = jnp.transpose(shaped, (4, 0, 2, 1, 3))
    return shaped.reshape(channels, patch_rows * patch_size, grid_width * patch_size)


def convolve(padded, conv_w):
    row_count = padded.shape[1] - 2
    col_count = padded.shape[2] - 2
    tap_list = [
        padded[:, tap_row : tap_row + row_count, tap_col : tap_col + col_count]
        for tap_row in range(3)
        for tap_col in range(3)
    ]
    stacked = jnp.stack(tap_list, axis=1).reshape(padded.shape[0] * 9, row_count * col_count)
    convolved = jnp.dot(conv_w, stacked, preferred_element_type=jnp.float32)
    return convolved.reshape(conv_w.shape[0], row_count, col_count)


def text_state(queries, keys_txt, vals_txt, length):
    text_allowed = (jnp.arange(keys_txt.shape[0], dtype=jnp.int32) < length)[None, None, :]
    text_scores = (
        jnp.einsum("qhd,khd->qhk", queries, keys_txt, preferred_element_type=jnp.float32)
        * SCORE_SCALE
    )
    text_scores = jnp.where(text_allowed, text_scores, NEG_LARGE)
    text_max = jnp.max(text_scores, axis=2)
    text_weights = jnp.where(text_allowed, jnp.exp(text_scores - text_max[:, :, None]), 0.0)
    text_acc = jnp.einsum(
        "qhk,khd->qhd",
        text_weights.astype(jnp.bfloat16),
        vals_txt,
        preferred_element_type=jnp.float32,
    )
    return (text_max, jnp.sum(text_weights, axis=2), text_acc)


def absorb_block(previous, queries, head_keys, head_vals, allowed):
    old_max, old_sum, old_acc = previous
    scores = (
        jnp.einsum("qhd,khd->qhk", queries, head_keys, preferred_element_type=jnp.float32)
        * SCORE_SCALE
    )
    scores = jnp.where(allowed, scores, NEG_LARGE)
    new_max = jnp.maximum(old_max, jnp.max(scores, axis=2))
    weights = jnp.where(allowed, jnp.exp(scores - new_max[:, :, None]), 0.0)
    factor = jnp.exp(old_max - new_max)
    summed = jnp.einsum(
        "qhk,khd->qhd", weights.astype(jnp.bfloat16), head_vals, preferred_element_type=jnp.float32
    )
    return (
        new_max,
        old_sum * factor + jnp.sum(weights, axis=2),
        old_acc * factor[:, :, None] + summed,
    )


def absorb_maybe(previous, queries, head_keys, head_vals, allowed):
    return absorb_block(previous, queries, head_keys, head_vals, allowed)


def on_device(
    x_img,
    x_txt,
    modulation,
    w_img,
    w_txt,
    w_out,
    w_final,
    lengths,
    block_mask,
    timestep,
    latent,
    conv_w,
):
    tokens = x_img[0]
    factors = modulation[0]
    tok_rows = tokens.shape[0]
    head_cols = w_out.shape[0] * lax.axis_size("req")
    head_count = head_cols // HD
    h_img = modulate(tokens, factors[0], factors[1]).astype(jnp.bfloat16)
    h_txt = modulate(x_txt[0], factors[3], factors[4]).astype(jnp.bfloat16)
    qkv = jnp.dot(
        h_img, lax.all_gather(w_img, "req", axis=1, tiled=True), preferred_element_type=jnp.float32
    ).astype(jnp.bfloat16)
    kv_txt = jnp.dot(
        h_txt, lax.all_gather(w_txt, "req", axis=1, tiled=True), preferred_element_type=jnp.float32
    ).astype(jnp.bfloat16)
    keys_txt = kv_txt[:, :head_cols].reshape(-1, head_count, HD)
    vals_txt = kv_txt[:, head_cols:].reshape(-1, head_count, HD)
    length = lengths[0]
    queries = qkv[:, :head_cols].reshape(tok_rows, head_count, HD)
    keys_img = qkv[:, head_cols : 2 * head_cols]
    vals_img = qkv[:, 2 * head_cols :]
    mask_row = block_mask[0, 0]
    tile_count = mask_row.shape[0]
    start_state = text_state(queries, keys_txt, vals_txt, length)
    piece_keys = lax.all_gather(keys_img, "blk", axis=0, tiled=True)
    piece_vals = lax.all_gather(vals_img, "blk", axis=0, tiled=True)
    piece_len = piece_keys.shape[0]
    key_tile = jnp.arange(piece_len, dtype=jnp.int32) // tok_rows
    tile_hit = key_tile[:, None] == jnp.arange(tile_count, dtype=jnp.int32)[None, :]
    allowed = jnp.sum(jnp.where(tile_hit, mask_row[None, :], 0), axis=1) == 1
    head_keys = piece_keys.reshape(piece_len, head_count, HD)
    head_vals = piece_vals.reshape(piece_len, head_count, HD)
    run_max, run_sum, run_acc = absorb_maybe(
        start_state, queries, head_keys, head_vals, allowed[None, None, :]
    )
    attended = (run_acc / run_sum[:, :, None]).reshape(tok_rows, head_cols).astype(jnp.bfloat16)
    projected = jnp.dot(
        attended,
        lax.all_gather(w_out, "req", axis=0, tiled=True),
        preferred_element_type=jnp.float32,
    )
    residual = tokens.astype(jnp.float32) + factors[2] * projected
    final_in = modulate(residual, factors[5], factors[6]).astype(jnp.bfloat16)
    token_out = jnp.dot(final_in, w_final, preferred_element_type=jnp.float32)
    velocity = unpatchify(token_out, GRIDW, PATCH, LATC)[None]
    step_index = timestep[0]
    sigma_step = sigma_of(step_index + 1, NSTEPS) - sigma_of(step_index, NSTEPS)
    latent_next = latent + sigma_step * velocity
    decoded = (latent_next / LATENT_SCALE + LATENT_SHIFT).astype(jnp.bfloat16)
    padded = with_halo(decoded, (("blk", 2),), 1)
    padded = jnp.pad(padded[0], ((0, 0), (0, 0), (1, 1)))
    features = convolve(padded, conv_w).astype(jnp.bfloat16)[None]
    return (velocity, latent_next, features)


MESH = pl.DeviceIdType.MESH
NTILE = 4
NREQ = 8
CHUNK = 96
TXT_PAD = 256
F32 = jnp.float32
BF16 = jnp.bfloat16


def nt_dot(a, b):
    return lax.dot_general(a, b, (((1,), (1,)), ((), ())), preferred_element_type=F32)


def flip(r, bit):
    return r + bit - 2 * bit * ((r // bit) % 2)


def normed(v):
    v = v.astype(F32)
    c = v - jnp.mean(v, axis=-1, keepdims=True)
    return c * lax.rsqrt(jnp.mean(c * c, axis=-1, keepdims=True) + NORM_EPS)


def kernel(
    x_ref, xt_ref, mod_ref, wi_ref, wt_ref, wo_ref, wf_ref, bias_ref, ss_ref, lat_ref,
    vel_ref, next_ref, stk_ref,
    H, HT, WI, WT, WO, Q, K, V, BIAS, A, AT, FIN, DEC,
    z_send, h_recv, b_send, b_recv, wi_send, wi_recv, wt_send, wt_recv,
    wo_send, wo_recv, a_send, a_recv, d_send, d_recv, l_sem,
):
    r = lax.axis_index("req")
    z = lax.axis_index("blk")
    rows = x_ref.shape[0]
    tokens = rows * NTILE
    group = WI.shape[0] // 3
    sib = flip(r, 1)
    nx = flip(r, 2)
    ny = flip(r, 4)
    nd = flip(nx, 4)

    def rcopy(src, dst, ss, rs, **dev):
        return pltpu.make_async_remote_copy(
            src_ref=src, dst_ref=dst, send_sem=ss, recv_sem=rs, device_id=dev, device_id_type=MESH
        )

    barrier = pltpu.get_barrier_semaphore()
    for step in range(1, NREQ):
        pl.semaphore_signal(
            barrier, inc=1, device_id={"req": lax.rem(r + step, NREQ)}, device_id_type=MESH
        )
    for step in range(1, NTILE):
        pl.semaphore_signal(
            barrier, inc=1, device_id={"blk": lax.rem(z + step, NTILE)}, device_id_type=MESH
        )
    pl.semaphore_wait(barrier, NREQ - 1 + NTILE - 1)

    pieces = []
    for j in range(6):
        via = j % 2
        cid = 8 * (j // 2) + 2 * z + j % 2
        off = pl.multiple_of((cid % 3) * CHUNK, CHUNK)
        pieces.append(
            (wi_ref.at[pl.ds(off, CHUNK)], WI.at[pl.ds(j * CHUNK, CHUNK)], cid // 3, via, wi_send.at[j], wi_recv.at[j], l_sem.at[j])
        )
    for j in range(4):
        part = pl.ds((j % 2) * CHUNK, CHUNK)
        pieces.append(
            (wt_ref.at[part], WT.at[pl.ds(j * CHUNK, CHUNK)], 4 * (j // 2) + z, j % 2, wt_send.at[j], wt_recv.at[j], l_sem.at[6 + j])
        )

    for src, slot, owner, via, ss, rs, ls in pieces:
        @pl.when(owner == r)
        def _():
            for n, dev in enumerate((nx, ny, sib)):
                rcopy(src, slot, ss.at[n], rs, req=dev).start()
            pltpu.make_async_copy(src, slot, ls).start()

    def norm_rows(i, src, dst, shift, scale):
        at = pl.ds(pl.multiple_of(i * 32, 32), 32)
        dst[at, :] = (normed(src[at, :]) * (1.0 + mod_ref[scale : scale + 1, :]) + mod_ref[shift : shift + 1, :]).astype(BF16)

    own = H.at[z]
    pl.loop(0, rows // 32)(lambda i: norm_rows(i, x_ref, own, 0, 1))

    def up(t):
        return rcopy(H.at[t], H.at[t], z_send.at[0, t], h_recv.at[t], blk=z + 1)

    def down(t):
        return rcopy(H.at[t], H.at[t], z_send.at[1, t], h_recv.at[t], blk=z - 1)

    @pl.when(z < NTILE - 1)
    def _():
        up(z).start()

    @pl.when(z > 0)
    def _():
        down(z).start()

    def take(step):
        low, high = z - step, z + step

        @pl.when(low >= 0)
        def _():
            rcopy(H.at[low], H.at[low], z_send.at[0, low], h_recv.at[low], blk=z).wait_recv()

            @pl.when(z < NTILE - 1)
            def _():
                up(low).start()

        @pl.when(high < NTILE)
        def _():
            rcopy(H.at[high], H.at[high], z_send.at[1, high], h_recv.at[high], blk=z).wait_recv()

            @pl.when(z > 0)
            def _():
                down(high).start()

    BIAS[z] = bias_ref[...]
    for step in range(1, NTILE):
        rcopy(BIAS.at[z], BIAS.at[z], b_send.at[step], b_recv.at[NTILE - step], blk=lax.rem(z + step, NTILE)).start()

    pl.loop(0, TXT_PAD // 32)(lambda i: norm_rows(i, xt_ref, HT, 3, 4))

    for src, slot, owner, via, ss, rs, ls in pieces:
        near, onward = ((nx, ny), (ny, nx))[via]

        @pl.when(jnp.logical_or(owner == nx, owner == ny))
        def _():
            rcopy(src, slot, ss.at[0], rs, req=sib).wait_recv()
            rcopy(slot, slot, ss.at[0], rs, req=sib).start()

        @pl.when(owner == near)
        def _():
            rcopy(slot, slot, ss.at[1], rs, req=onward).start()

    take(1)

    for src, slot, owner, via, ss, rs, ls in pieces:
        @pl.when(owner == r)
        def _():
            pltpu.make_async_copy(src, slot, ls).wait()

        @pl.when(owner == nd)
        def _():
            rcopy(src, slot, ss.at[0], rs, req=sib).wait_recv()
            rcopy(slot, slot, ss.at[0], rs, req=sib).start()

        @pl.when(owner % 2 != r % 2)
        def _():
            rcopy(src, slot, ss.at[0], rs, req=sib).wait_recv()

    def wo_rows(dev):
        return WO.at[pl.ds(pl.multiple_of(dev * CHUNK, CHUNK), CHUNK)]

    for n, (k, dev) in enumerate(((2, nx), (4, ny), (6, nd), (1, sib))):
        rcopy(wo_ref, wo_rows(r), wo_send.at[n], wo_recv.at[k], req=dev).start()
    pltpu.make_async_copy(wo_ref, wo_rows(r), l_sem.at[10]).start()

    kv = nt_dot(HT[...], WT[...]).astype(BF16)
    K[tokens:, :] = kv[:, :group]
    V[tokens:, :] = kv[:, group:]

    def project(t):
        at = pl.ds(pl.multiple_of(t * rows, rows), rows)
        qkv = nt_dot(H[t], WI[...]).astype(BF16)
        Q[at, :] = qkv[:, :group] * jnp.asarray(SCORE_SCALE, BF16)
        K[at, :] = qkv[:, group : 2 * group]
        V[at, :] = qkv[:, 2 * group :]

    project(z)
    for step in range(1, NTILE):
        low, high = z - step, z + step
        if step > 1:
            take(step)
        if step == 2:
            for n, (k, dev) in enumerate(((2, nx), (4, ny), (6, nd))):
                rows_of = wo_rows(dev)
                rcopy(wo_ref, rows_of, wo_send.at[n], wo_recv.at[k], req=sib).wait_recv()
                rcopy(rows_of, rows_of, wo_send.at[4 + n], wo_recv.at[k + 1], req=sib).start()

        @pl.when(low >= 0)
        def _():
            project(low)

        @pl.when(high < NTILE)
        def _():
            project(high)

    for step in range(1, NTILE):
        src = BIAS.at[lax.rem(z + step, NTILE)]
        rcopy(src, src, b_send.at[step], b_recv.at[step], blk=lax.rem(z + step, NTILE)).wait_recv()

    def attend(t):
        at = pl.ds(pl.multiple_of(t * rows, rows), rows)
        bias = BIAS[t][0:1, :]
        q, k, v = Q[at, :], K[...], V[...]
        outs = []
        for h in range(group // HD):
            cols = slice(h * HD, (h + 1) * HD)
            s = nt_dot(q[:, cols], k[:, cols]) + bias
            p = jnp.exp(s - jnp.max(s, axis=1, keepdims=True))
            total = jnp.sum(p, axis=1, keepdims=True)
            o = jnp.dot(p.astype(BF16), v[:, cols], preferred_element_type=F32)
            outs.append(o / total)
        return jnp.concatenate(outs, axis=1).astype(BF16)

    for step in range(1, NTILE):
        t = lax.rem(z + step, NTILE)
        A[step] = attend(t)
        rcopy(A.at[step], AT.at[z], a_send.at[step], a_recv.at[NTILE - step], blk=t).start()
    AT[z] = attend(z)

    pltpu.make_async_copy(wo_ref, wo_rows(r), l_sem.at[10]).wait()
    rcopy(wo_ref, wo_rows(sib), wo_send.at[3], wo_recv.at[1], req=sib).wait_recv()
    for n, (k, dev) in enumerate(((3, nx), (5, ny), (7, nd))):
        rcopy(wo_ref, wo_rows(flip(dev, 1)), wo_send.at[4 + n], wo_recv.at[k], req=sib).wait_recv()
    for step in range(1, NTILE):
        src = AT.at[lax.rem(z + step, NTILE)]
        rcopy(src, src, a_send.at[step], a_recv.at[step], blk=lax.rem(z + step, NTILE)).wait_recv()

    def out_rows(i):
        at = pl.ds(pl.multiple_of(i * 64, 64), 64)
        proj = jnp.dot(AT[0, at, :], WO[0:group, :], preferred_element_type=F32)
        for s in range(1, NTILE):
            proj += jnp.dot(AT[s, at, :], WO[s * group : (s + 1) * group, :], preferred_element_type=F32)
        res = x_ref[at, :].astype(F32) + mod_ref[2:3, :] * proj
        FIN[at, :] = (normed(res) * (1.0 + mod_ref[6:7, :]) + mod_ref[5:6, :]).astype(BF16)

    pl.loop(0, rows // 64)(out_rows)

    dup = (
        lax.broadcasted_iota(jnp.int32, (2 * rows, rows), 0) // 2
        == lax.broadcasted_iota(jnp.int32, (2 * rows, rows), 1)
    ).astype(F32).astype(BF16)
    twice = jnp.dot(dup, FIN[...], preferred_element_type=F32).astype(BF16)
    tok = jnp.dot(twice, wf_ref[...], preferred_element_type=F32).T
    even = lax.broadcasted_iota(jnp.int32, (LATC, 2 * rows), 1) % 2 == 0
    width = PATCH * GRIDW
    sig = ss_ref[0:1, :]
    for p in range(PATCH):
        base = p * 2 * LATC
        val = jnp.where(even, tok[base : base + LATC], tok[base + LATC : base + 2 * LATC])
        for a in range(rows // GRIDW):
            y = PATCH * a + p
            piece = val[:, a * width : (a + 1) * width]
            nxt = lat_ref[:, y, :] + sig * piece
            vel_ref[:, y, :] = piece
            next_ref[:, y, :] = nxt
            DEC[y + 1] = (nxt / LATENT_SCALE + LATENT_SHIFT).astype(BF16)

    count = PATCH * rows // GRIDW
    go_up = rcopy(DEC.at[count], DEC.at[0], d_send.at[0], d_recv.at[0], blk=z + 1)
    go_down = rcopy(DEC.at[1], DEC.at[count + 1], d_send.at[1], d_recv.at[1], blk=z - 1)

    @pl.when(z < NTILE - 1)
    def _():
        go_up.start()

    @pl.when(z > 0)
    def _():
        go_down.start()

    @pl.when(z == 0)
    def _():
        DEC[0] = jnp.zeros((LATC, width), BF16)

    @pl.when(z == NTILE - 1)
    def _():
        DEC[count + 1] = jnp.zeros((LATC, width), BF16)

    for src, slot, owner, via, ss, rs, ls in pieces:
        near = (nx, ny)[via]

        @pl.when(owner == r)
        def _():
            for n in range(3):
                rcopy(src, slot, ss.at[n], rs, req=sib).wait_send()

        @pl.when(jnp.logical_and(owner != r, owner % 2 == r % 2))
        def _():
            rcopy(slot, slot, ss.at[0], rs, req=sib).wait_send()

        @pl.when(owner == near)
        def _():
            rcopy(slot, slot, ss.at[1], rs, req=sib).wait_send()

    for n in range(7):
        rcopy(wo_ref, wo_rows(r), wo_send.at[n], wo_recv.at[1], req=sib).wait_send()
    for t in range(NTILE):
        @pl.when(jnp.logical_and(z < NTILE - 1, t <= z))
        def _():
            up(t).wait_send()

        @pl.when(jnp.logical_and(z > 0, t >= z))
        def _():
            down(t).wait_send()
    for step in range(1, NTILE):
        there = lax.rem(z + step, NTILE)
        rcopy(BIAS.at[z], BIAS.at[z], b_send.at[step], b_recv.at[step], blk=there).wait_send()
        rcopy(A.at[step], AT.at[z], a_send.at[step], a_recv.at[step], blk=there).wait_send()

    @pl.when(z < NTILE - 1)
    def _():
        go_up.wait_send()
        go_down.wait_recv()

    @pl.when(z > 0)
    def _():
        go_down.wait_send()
        go_up.wait_recv()

    lane = lax.broadcasted_iota(jnp.int32, (LATC, width), 1)
    for yy in range(count + 2):
        mid = DEC[yy].astype(F32)
        shifted = (
            jnp.where(lane == 0, 0.0, pltpu.roll(mid, 1, 1)),
            mid,
            jnp.where(lane == width - 1, 0.0, pltpu.roll(mid, width - 1, 1)),
        )
        for a in range(3):
            y = yy - a
            if 0 <= y < count:
                for b in range(3):
                    at = (3 * a + b) * LATC
                    stk_ref[at : at + LATC, y * width : (y + 1) * width] = shifted[b].astype(BF16)


def split_heads(
    x_img, x_txt, modulation, w_img, w_txt, w_out, w_final, lengths, block_mask, timestep, latent, conv_w
):
    rows, model = x_img.shape[1], x_img.shape[2]
    group = w_out.shape[0] * NREQ // NTILE
    tokens = rows * NTILE
    allowed = jnp.concatenate(
        [jnp.repeat(block_mask[0, 0] == 1, rows), jnp.arange(TXT_PAD, dtype=jnp.int32) < lengths[0]]
    )
    bias = jnp.broadcast_to(jnp.where(allowed, 0.0, NEG_LARGE).astype(F32)[None, :], (8, tokens + TXT_PAD))
    step_index = timestep[0]
    sigma_step = sigma_of(step_index + 1, NSTEPS) - sigma_of(step_index, NSTEPS)
    height, width = latent.shape[2], latent.shape[3]
    xt = jnp.pad(x_txt[0], ((0, TXT_PAD - x_txt.shape[1]), (0, 0)))
    vmem = pl.BlockSpec(memory_space=pltpu.VMEM)
    hbm = pl.BlockSpec(memory_space=pl.ANY)
    dma = pltpu.SemaphoreType.DMA
    velocity, latent_next, stacked = pl.pallas_call(
        kernel,
        out_shape=(
            jax.ShapeDtypeStruct((LATC, height, width), F32),
            jax.ShapeDtypeStruct((LATC, height, width), F32),
            jax.ShapeDtypeStruct((9 * LATC, height * width), BF16),
        ),
        in_specs=[vmem, vmem, vmem, hbm, hbm, hbm, vmem, vmem, vmem, vmem],
        out_specs=(vmem, vmem, vmem),
        scratch_shapes=[
            pltpu.VMEM((NTILE, rows, model), BF16),
            pltpu.VMEM((TXT_PAD, model), BF16),
            pltpu.VMEM((3 * group, model), BF16),
            pltpu.VMEM((2 * group, model), BF16),
            pltpu.VMEM((NTILE * group, model), BF16),
            pltpu.VMEM((tokens, group), BF16),
            pltpu.VMEM((tokens + TXT_PAD, group), BF16),
            pltpu.VMEM((tokens + TXT_PAD, group), BF16),
            pltpu.VMEM((NTILE, 8, tokens + TXT_PAD), F32),
            pltpu.VMEM((NTILE, rows, group), BF16),
            pltpu.VMEM((NTILE, rows, group), BF16),
            pltpu.VMEM((rows, model), BF16),
            pltpu.VMEM((height + 2, LATC, width), BF16),
            dma((2, NTILE)),
            dma((NTILE,)),
            dma((NTILE,)),
            dma((NTILE,)),
            dma((6, 4)),
            dma((6,)),
            dma((4, 4)),
            dma((4,)),
            dma((7,)),
            dma((8,)),
            dma((NTILE,)),
            dma((NTILE,)),
            dma((2,)),
            dma((2,)),
            dma((11,)),
        ],
        compiler_params=pltpu.CompilerParams(
            collective_id=0, has_side_effects=True, vmem_limit_bytes=48 * 1024 * 1024
        ),
        name="split_heads",
    )(
        x_img[0], xt, modulation[0], w_img.T, w_txt.T, w_out, w_final, bias,
        jnp.full((8, width), sigma_step, F32), latent[0],
    )
    taps = conv_w.reshape(-1, LATC, 9).transpose(0, 2, 1).reshape(-1, 9 * LATC)
    features = jnp.dot(taps, stacked, preferred_element_type=F32).astype(BF16)
    return velocity[None], latent_next[None], features.reshape(1, -1, height, width)


def solution(mesh):
    fits = mesh.shape["blk"] == NTILE and mesh.shape["req"] == NREQ
    return jax.shard_map(
        split_heads if fits else on_device,
        mesh=mesh,
        in_specs=(
            P("req", "blk", None),
            P("req", None, None),
            P("req", None, None),
            P(None, "req"),
            P(None, "req"),
            P("req", None),
            P(),
            P("req"),
            P("req", "blk", None),
            P("req"),
            P("req", None, "blk", None),
            P(),
        ),
        out_specs=(
            P("req", None, "blk", None),
            P("req", None, "blk", None),
            P("req", None, "blk", None),
        ),
        check_vma=False,
    )
```

```python
import jax
import jax.numpy as jnp
from jax import lax
from jax.experimental import pallas as pl
from jax.experimental.pallas import tpu as pltpu
from jax.sharding import PartitionSpec as P

HD = 64
GRIDW = 64
PATCH = 2
LATC = 16
NSTEPS = 28


NORM_EPS = 1e-06
SHIFT_FACTOR = 3.0
LATENT_SCALE = 1.5305
LATENT_SHIFT = 0.0609
NEG_LARGE = -1e30
SCORE_SCALE = 0.125


def with_halo(block, sides, width):
    for axis, dim in sides:
        count = lax.axis_size(axis)
        forward = [(i, i + 1) for i in range(count - 1)]
        backward = [(target, source) for source, target in forward]
        low = lax.ppermute(
            lax.slice_in_dim(block, block.shape[dim] - width, None, axis=dim), axis, forward
        )
        high = lax.ppermute(lax.slice_in_dim(block, 0, width, axis=dim), axis, backward)
        block = jnp.concatenate([low, block, high], axis=dim)
    return block


def layer_norm(values):
    values = values.astype(jnp.float32)
    center = values - jnp.mean(values, axis=-1, keepdims=True)
    spread = jnp.mean(center * center, axis=-1, keepdims=True)
    return center * lax.rsqrt(spread + NORM_EPS)


def modulate(values, shift_row, scale_row):
    return layer_norm(values) * (1.0 + scale_row) + shift_row


def sigma_of(step_index, step_count):
    fraction = 1.0 - step_index.astype(jnp.float32) / step_count
    return SHIFT_FACTOR * fraction / (1.0 + (SHIFT_FACTOR - 1.0) * fraction)


def unpatchify(token_out, grid_width, patch_size, channels):
    patch_rows = token_out.shape[0] // grid_width
    shaped = token_out.reshape(patch_rows, grid_width, patch_size, patch_size, channels)
    shaped = jnp.transpose(shaped, (4, 0, 2, 1, 3))
    return shaped.reshape(channels, patch_rows * patch_size, grid_width * patch_size)


def convolve(padded, conv_w):
    row_count = padded.shape[1] - 2
    col_count = padded.shape[2] - 2
    tap_list = [
        padded[:, tap_row : tap_row + row_count, tap_col : tap_col + col_count]
        for tap_row in range(3)
        for tap_col in range(3)
    ]
    stacked = jnp.stack(tap_list, axis=1).reshape(padded.shape[0] * 9, row_count * col_count)
    convolved = jnp.dot(conv_w, stacked, preferred_element_type=jnp.float32)
    return convolved.reshape(conv_w.shape[0], row_count, col_count)


def text_state(queries, keys_txt, vals_txt, length):
    text_allowed = (jnp.arange(keys_txt.shape[0], dtype=jnp.int32) < length)[None, None, :]
    text_scores = (
        jnp.einsum("qhd,khd->qhk", queries, keys_txt, preferred_element_type=jnp.float32)
        * SCORE_SCALE
    )
    text_scores = jnp.where(text_allowed, text_scores, NEG_LARGE)
    text_max = jnp.max(text_scores, axis=2)
    text_weights = jnp.where(text_allowed, jnp.exp(text_scores - text_max[:, :, None]), 0.0)
    text_acc = jnp.einsum(
        "qhk,khd->qhd",
        text_weights.astype(jnp.bfloat16),
        vals_txt,
        preferred_element_type=jnp.float32,
    )
    return (text_max, jnp.sum(text_weights, axis=2), text_acc)


def absorb_block(previous, queries, head_keys, head_vals, allowed):
    old_max, old_sum, old_acc = previous
    scores = (
        jnp.einsum("qhd,khd->qhk", queries, head_keys, preferred_element_type=jnp.float32)
        * SCORE_SCALE
    )
    scores = jnp.where(allowed, scores, NEG_LARGE)
    new_max = jnp.maximum(old_max, jnp.max(scores, axis=2))
    weights = jnp.where(allowed, jnp.exp(scores - new_max[:, :, None]), 0.0)
    factor = jnp.exp(old_max - new_max)
    summed = jnp.einsum(
        "qhk,khd->qhd", weights.astype(jnp.bfloat16), head_vals, preferred_element_type=jnp.float32
    )
    return (
        new_max,
        old_sum * factor + jnp.sum(weights, axis=2),
        old_acc * factor[:, :, None] + summed,
    )


def absorb_maybe(previous, queries, head_keys, head_vals, allowed):
    return absorb_block(previous, queries, head_keys, head_vals, allowed)


def on_device(
    x_img,
    x_txt,
    modulation,
    w_img,
    w_txt,
    w_out,
    w_final,
    lengths,
    block_mask,
    timestep,
    latent,
    conv_w,
):
    tokens = x_img[0]
    factors = modulation[0]
    tok_rows = tokens.shape[0]
    head_cols = w_out.shape[0] * lax.axis_size("req")
    head_count = head_cols // HD
    h_img = modulate(tokens, factors[0], factors[1]).astype(jnp.bfloat16)
    h_txt = modulate(x_txt[0], factors[3], factors[4]).astype(jnp.bfloat16)
    qkv = jnp.dot(
        h_img, lax.all_gather(w_img, "req", axis=1, tiled=True), preferred_element_type=jnp.float32
    ).astype(jnp.bfloat16)
    kv_txt = jnp.dot(
        h_txt, lax.all_gather(w_txt, "req", axis=1, tiled=True), preferred_element_type=jnp.float32
    ).astype(jnp.bfloat16)
    keys_txt = kv_txt[:, :head_cols].reshape(-1, head_count, HD)
    vals_txt = kv_txt[:, head_cols:].reshape(-1, head_count, HD)
    length = lengths[0]
    queries = qkv[:, :head_cols].reshape(tok_rows, head_count, HD)
    keys_img = qkv[:, head_cols : 2 * head_cols]
    vals_img = qkv[:, 2 * head_cols :]
    mask_row = block_mask[0, 0]
    tile_count = mask_row.shape[0]
    start_state = text_state(queries, keys_txt, vals_txt, length)
    piece_keys = lax.all_gather(keys_img, "blk", axis=0, tiled=True)
    piece_vals = lax.all_gather(vals_img, "blk", axis=0, tiled=True)
    piece_len = piece_keys.shape[0]
    key_tile = jnp.arange(piece_len, dtype=jnp.int32) // tok_rows
    tile_hit = key_tile[:, None] == jnp.arange(tile_count, dtype=jnp.int32)[None, :]
    allowed = jnp.sum(jnp.where(tile_hit, mask_row[None, :], 0), axis=1) == 1
    head_keys = piece_keys.reshape(piece_len, head_count, HD)
    head_vals = piece_vals.reshape(piece_len, head_count, HD)
    run_max, run_sum, run_acc = absorb_maybe(
        start_state, queries, head_keys, head_vals, allowed[None, None, :]
    )
    attended = (run_acc / run_sum[:, :, None]).reshape(tok_rows, head_cols).astype(jnp.bfloat16)
    projected = jnp.dot(
        attended,
        lax.all_gather(w_out, "req", axis=0, tiled=True),
        preferred_element_type=jnp.float32,
    )
    residual = tokens.astype(jnp.float32) + factors[2] * projected
    final_in = modulate(residual, factors[5], factors[6]).astype(jnp.bfloat16)
    token_out = jnp.dot(final_in, w_final, preferred_element_type=jnp.float32)
    velocity = unpatchify(token_out, GRIDW, PATCH, LATC)[None]
    step_index = timestep[0]
    sigma_step = sigma_of(step_index + 1, NSTEPS) - sigma_of(step_index, NSTEPS)
    latent_next = latent + sigma_step * velocity
    decoded = (latent_next / LATENT_SCALE + LATENT_SHIFT).astype(jnp.bfloat16)
    padded = with_halo(decoded, (("blk", 2),), 1)
    padded = jnp.pad(padded[0], ((0, 0), (0, 0), (1, 1)))
    features = convolve(padded, conv_w).astype(jnp.bfloat16)[None]
    return (velocity, latent_next, features)


MESH = pl.DeviceIdType.MESH
NTILE = 4
NREQ = 8
CHUNK = 96
TXT_PAD = 256
F32 = jnp.float32
BF16 = jnp.bfloat16


def nt_dot(a, b):
    return lax.dot_general(a, b, (((1,), (1,)), ((), ())), preferred_element_type=F32)


def flip(r, bit):
    return r + bit - 2 * bit * ((r // bit) % 2)


def normed(v):
    v = v.astype(F32)
    c = v - jnp.mean(v, axis=-1, keepdims=True)
    return c * lax.rsqrt(jnp.mean(c * c, axis=-1, keepdims=True) + NORM_EPS)


def kernel(
    x_ref, xt_ref, mod_ref, wi_ref, wt_ref, wo_ref, wf_ref, bias_ref, ss_ref, lat_ref,
    vel_ref, next_ref, stk_ref,
    H, HT, WI, WT, WO, Q, K, V, BIAS, A, AT, FIN, DEC, STK,
    z_send, h_recv, b_send, b_recv, wi_send, wi_recv, wt_send, wt_recv,
    wo_send, wo_recv, a_send, a_recv, d_send, d_recv, l_sem,
):
    r = lax.axis_index("req")
    z = lax.axis_index("blk")
    rows = x_ref.shape[0]
    tokens = rows * NTILE
    group = WI.shape[0] // 3
    sib = flip(r, 1)
    nx = flip(r, 2)
    ny = flip(r, 4)
    nd = flip(nx, 4)

    def rcopy(src, dst, ss, rs, **dev):
        return pltpu.make_async_remote_copy(
            src_ref=src, dst_ref=dst, send_sem=ss, recv_sem=rs, device_id=dev, device_id_type=MESH
        )

    barrier = pltpu.get_barrier_semaphore()
    for step in range(1, NREQ):
        pl.semaphore_signal(
            barrier, inc=1, device_id={"req": lax.rem(r + step, NREQ)}, device_id_type=MESH
        )
    for step in range(1, NTILE):
        pl.semaphore_signal(
            barrier, inc=1, device_id={"blk": lax.rem(z + step, NTILE)}, device_id_type=MESH
        )
    pl.semaphore_wait(barrier, NREQ - 1 + NTILE - 1)

    pieces = []
    for j in range(6):
        via = j % 2
        cid = 8 * (j // 2) + 2 * z + j % 2
        off = pl.multiple_of((cid % 3) * CHUNK, CHUNK)
        pieces.append(
            (wi_ref.at[pl.ds(off, CHUNK)], WI.at[pl.ds(j * CHUNK, CHUNK)], cid // 3, via, wi_send.at[j], wi_recv.at[j], l_sem.at[j])
        )
    for j in range(4):
        part = pl.ds((j % 2) * CHUNK, CHUNK)
        pieces.append(
            (wt_ref.at[part], WT.at[pl.ds(j * CHUNK, CHUNK)], 4 * (j // 2) + z, j % 2, wt_send.at[j], wt_recv.at[j], l_sem.at[6 + j])
        )

    for src, slot, owner, via, ss, rs, ls in pieces:
        @pl.when(owner == r)
        def _():
            for n, dev in enumerate((nx, ny, sib)):
                rcopy(src, slot, ss.at[n], rs, req=dev).start()
            pltpu.make_async_copy(src, slot, ls).start()

    def norm_rows(i, src, dst, shift, scale):
        at = pl.ds(pl.multiple_of(i * 32, 32), 32)
        dst[at, :] = (normed(src[at, :]) * (1.0 + mod_ref[scale]) + mod_ref[shift]).astype(BF16)

    own = H.at[z]
    pl.loop(0, rows // 32)(lambda i: norm_rows(i, x_ref, own, 0, 1))

    def up(t):
        return rcopy(H.at[t], H.at[t], z_send.at[0, t], h_recv.at[t], blk=z + 1)

    def down(t):
        return rcopy(H.at[t], H.at[t], z_send.at[1, t], h_recv.at[t], blk=z - 1)

    @pl.when(z < NTILE - 1)
    def _():
        up(z).start()

    @pl.when(z > 0)
    def _():
        down(z).start()

    def take(step):
        low, high = z - step, z + step

        @pl.when(low >= 0)
        def _():
            rcopy(H.at[low], H.at[low], z_send.at[0, low], h_recv.at[low], blk=z).wait_recv()

            @pl.when(z < NTILE - 1)
            def _():
                up(low).start()

        @pl.when(high < NTILE)
        def _():
            rcopy(H.at[high], H.at[high], z_send.at[1, high], h_recv.at[high], blk=z).wait_recv()

            @pl.when(z > 0)
            def _():
                down(high).start()

    BIAS[z] = bias_ref[...]
    for step in range(1, NTILE):
        rcopy(BIAS.at[z], BIAS.at[z], b_send.at[step], b_recv.at[NTILE - step], blk=lax.rem(z + step, NTILE)).start()

    whole = xt_ref.shape[0] // 32 * 32
    pl.loop(0, whole // 32)(lambda i: norm_rows(i, xt_ref, HT, 3, 4))
    rest = (normed(xt_ref[whole:, :]) * (1.0 + mod_ref[4]) + mod_ref[3]).astype(BF16)
    filler = jnp.zeros((TXT_PAD - xt_ref.shape[0], rest.shape[1]), BF16)
    HT[whole:, :] = jnp.concatenate([rest, filler], axis=0)

    for src, slot, owner, via, ss, rs, ls in pieces:
        near, onward = ((nx, ny), (ny, nx))[via]

        @pl.when(jnp.logical_or(owner == nx, owner == ny))
        def _():
            rcopy(src, slot, ss.at[0], rs, req=sib).wait_recv()
            rcopy(slot, slot, ss.at[0], rs, req=sib).start()

        @pl.when(owner == near)
        def _():
            rcopy(slot, slot, ss.at[1], rs, req=onward).start()

    take(1)

    for src, slot, owner, via, ss, rs, ls in pieces:
        @pl.when(owner == r)
        def _():
            pltpu.make_async_copy(src, slot, ls).wait()

        @pl.when(owner == nd)
        def _():
            rcopy(src, slot, ss.at[0], rs, req=sib).wait_recv()
            rcopy(slot, slot, ss.at[0], rs, req=sib).start()

        @pl.when(owner % 2 != r % 2)
        def _():
            rcopy(src, slot, ss.at[0], rs, req=sib).wait_recv()

    def wo_rows(dev):
        return WO.at[pl.ds(pl.multiple_of(dev * CHUNK, CHUNK), CHUNK)]

    for n, (k, dev) in enumerate(((2, nx), (4, ny), (6, nd), (1, sib))):
        rcopy(wo_ref, wo_rows(r), wo_send.at[n], wo_recv.at[k], req=dev).start()
    pltpu.make_async_copy(wo_ref, wo_rows(r), l_sem.at[10]).start()

    kv = nt_dot(HT[...], WT[...]).astype(BF16)
    K[tokens:, :] = kv[:, :group]
    V[tokens:, :] = kv[:, group:]

    def project(t):
        at = pl.ds(pl.multiple_of(t * rows, rows), rows)
        qkv = nt_dot(H[t], WI[...]).astype(BF16)
        Q[at, :] = qkv[:, :group] * jnp.asarray(SCORE_SCALE, BF16)
        K[at, :] = qkv[:, group : 2 * group]
        V[at, :] = qkv[:, 2 * group :]

    project(z)
    for step in range(1, NTILE):
        low, high = z - step, z + step
        if step > 1:
            take(step)
        if step == 2:
            for n, (k, dev) in enumerate(((2, nx), (4, ny), (6, nd))):
                rows_of = wo_rows(dev)
                rcopy(wo_ref, rows_of, wo_send.at[n], wo_recv.at[k], req=sib).wait_recv()
                rcopy(rows_of, rows_of, wo_send.at[4 + n], wo_recv.at[k + 1], req=sib).start()

        @pl.when(low >= 0)
        def _():
            project(low)

        @pl.when(high < NTILE)
        def _():
            project(high)

    for step in range(1, NTILE):
        src = BIAS.at[lax.rem(z + step, NTILE)]
        rcopy(src, src, b_send.at[step], b_recv.at[step], blk=lax.rem(z + step, NTILE)).wait_recv()

    def attend(t):
        at = pl.ds(pl.multiple_of(t * rows, rows), rows)
        bias = BIAS[t][0:1, :]
        q, k, v = Q[at, :], K[...], V[...]
        outs = []
        for h in range(group // HD):
            cols = slice(h * HD, (h + 1) * HD)
            s = nt_dot(q[:, cols], k[:, cols]) + bias
            p = jnp.exp(s - jnp.max(s, axis=1, keepdims=True))
            total = jnp.sum(p, axis=1, keepdims=True)
            o = jnp.dot(p.astype(BF16), v[:, cols], preferred_element_type=F32)
            outs.append(o / total)
        return jnp.concatenate(outs, axis=1).astype(BF16)

    for step in range(1, NTILE):
        t = lax.rem(z + step, NTILE)
        A[step] = attend(t)
        rcopy(A.at[step], AT.at[z], a_send.at[step], a_recv.at[NTILE - step], blk=t).start()
    AT[z] = attend(z)

    pltpu.make_async_copy(wo_ref, wo_rows(r), l_sem.at[10]).wait()
    rcopy(wo_ref, wo_rows(sib), wo_send.at[3], wo_recv.at[1], req=sib).wait_recv()
    for n, (k, dev) in enumerate(((3, nx), (5, ny), (7, nd))):
        rcopy(wo_ref, wo_rows(flip(dev, 1)), wo_send.at[4 + n], wo_recv.at[k], req=sib).wait_recv()
    for step in range(1, NTILE):
        src = AT.at[lax.rem(z + step, NTILE)]
        rcopy(src, src, a_send.at[step], a_recv.at[step], blk=lax.rem(z + step, NTILE)).wait_recv()

    def out_rows(i):
        at = pl.ds(pl.multiple_of(i * 64, 64), 64)
        proj = jnp.dot(AT[0, at, :], WO[0:group, :], preferred_element_type=F32)
        for s in range(1, NTILE):
            proj += jnp.dot(AT[s, at, :], WO[s * group : (s + 1) * group, :], preferred_element_type=F32)
        res = x_ref[at, :].astype(F32) + mod_ref[2] * proj
        FIN[at, :] = (normed(res) * (1.0 + mod_ref[6]) + mod_ref[5]).astype(BF16)

    pl.loop(0, rows // 64)(out_rows)

    dup = (
        lax.broadcasted_iota(jnp.int32, (2 * rows, rows), 0) // 2
        == lax.broadcasted_iota(jnp.int32, (2 * rows, rows), 1)
    ).astype(F32).astype(BF16)
    twice = jnp.dot(dup, FIN[...], preferred_element_type=F32).astype(BF16)
    tok = nt_dot(wf_ref[...], twice)
    even = lax.broadcasted_iota(jnp.int32, (LATC, 2 * rows), 1) % 2 == 0
    width = PATCH * GRIDW
    sig = ss_ref[0:1, :]
    for p in range(PATCH):
        base = p * 2 * LATC
        val = jnp.where(even, tok[base : base + LATC], tok[base + LATC : base + 2 * LATC])
        for a in range(rows // GRIDW):
            y = PATCH * a + p
            piece = val[:, a * width : (a + 1) * width]
            nxt = lat_ref[:, y, :] + sig * piece
            vel_ref[:, y, :] = piece
            next_ref[:, y, :] = nxt
            DEC[y + 1] = (nxt / LATENT_SCALE + LATENT_SHIFT).astype(BF16)

    count = PATCH * rows // GRIDW
    go_up = rcopy(DEC.at[count], DEC.at[0], d_send.at[0], d_recv.at[0], blk=z + 1)
    go_down = rcopy(DEC.at[1], DEC.at[count + 1], d_send.at[1], d_recv.at[1], blk=z - 1)

    @pl.when(z < NTILE - 1)
    def _():
        go_up.start()

    @pl.when(z > 0)
    def _():
        go_down.start()

    @pl.when(z == 0)
    def _():
        DEC[0] = jnp.zeros((LATC, width), BF16)

    @pl.when(z == NTILE - 1)
    def _():
        DEC[count + 1] = jnp.zeros((LATC, width), BF16)

    for src, slot, owner, via, ss, rs, ls in pieces:
        near = (nx, ny)[via]

        @pl.when(owner == r)
        def _():
            for n in range(3):
                rcopy(src, slot, ss.at[n], rs, req=sib).wait_send()

        @pl.when(jnp.logical_and(owner != r, owner % 2 == r % 2))
        def _():
            rcopy(slot, slot, ss.at[0], rs, req=sib).wait_send()

        @pl.when(owner == near)
        def _():
            rcopy(slot, slot, ss.at[1], rs, req=sib).wait_send()

    for n in range(7):
        rcopy(wo_ref, wo_rows(r), wo_send.at[n], wo_recv.at[1], req=sib).wait_send()
    for t in range(NTILE):
        @pl.when(jnp.logical_and(z < NTILE - 1, t <= z))
        def _():
            up(t).wait_send()

        @pl.when(jnp.logical_and(z > 0, t >= z))
        def _():
            down(t).wait_send()
    for step in range(1, NTILE):
        there = lax.rem(z + step, NTILE)
        rcopy(BIAS.at[z], BIAS.at[z], b_send.at[step], b_recv.at[step], blk=there).wait_send()
        rcopy(A.at[step], AT.at[z], a_send.at[step], a_recv.at[step], blk=there).wait_send()

    @pl.when(z < NTILE - 1)
    def _():
        go_up.wait_send()
        go_down.wait_recv()

    @pl.when(z > 0)
    def _():
        go_down.wait_send()
        go_up.wait_recv()

    lane = lax.broadcasted_iota(jnp.int32, (LATC, width), 1)
    for yy in range(count + 2):
        mid = DEC[yy].astype(F32)
        shifted = (
            jnp.where(lane == 0, 0.0, pltpu.roll(mid, 1, 1)),
            mid,
            jnp.where(lane == width - 1, 0.0, pltpu.roll(mid, width - 1, 1)),
        )
        for a in range(3):
            y = yy - a
            if 0 <= y < count:
                for b in range(3):
                    at = (3 * a + b) * LATC
                    STK[at : at + LATC, y * width : (y + 1) * width] = shifted[b].astype(BF16)

    taps = 9 * LATC
    row = lax.broadcasted_iota(jnp.int32, (taps, taps), 0)
    col = lax.broadcasted_iota(jnp.int32, (taps, taps), 1)
    order = (row == (col % LATC) * 9 + col // LATC).astype(F32).astype(BF16)
    stk_ref[...] = jnp.dot(order, STK[...], preferred_element_type=F32).astype(BF16)


def split_heads(
    x_img, x_txt, modulation, w_img, w_txt, w_out, w_final, lengths, block_mask, timestep, latent, conv_w
):
    rows, model = x_img.shape[1], x_img.shape[2]
    group = w_out.shape[0] * NREQ // NTILE
    tokens = rows * NTILE
    allowed = jnp.concatenate(
        [jnp.repeat(block_mask[0, 0] == 1, rows), jnp.arange(TXT_PAD, dtype=jnp.int32) < lengths[0]]
    )
    bias = jnp.broadcast_to(jnp.where(allowed, 0.0, NEG_LARGE).astype(F32)[None, :], (8, tokens + TXT_PAD))
    step_index = timestep[0]
    sigma_step = sigma_of(step_index + 1, NSTEPS) - sigma_of(step_index, NSTEPS)
    height, width = latent.shape[2], latent.shape[3]
    vmem = pl.BlockSpec(memory_space=pltpu.VMEM)
    hbm = pl.BlockSpec(memory_space=pl.ANY)
    dma = pltpu.SemaphoreType.DMA
    velocity, latent_next, stacked = pl.pallas_call(
        kernel,
        out_shape=(
            jax.ShapeDtypeStruct((LATC, height, width), F32),
            jax.ShapeDtypeStruct((LATC, height, width), F32),
            jax.ShapeDtypeStruct((9 * LATC, height * width), BF16),
        ),
        in_specs=[vmem, vmem, vmem, hbm, hbm, hbm, vmem, vmem, vmem, vmem],
        out_specs=(vmem, vmem, vmem),
        scratch_shapes=[
            pltpu.VMEM((NTILE, rows, model), BF16),
            pltpu.VMEM((TXT_PAD, model), BF16),
            pltpu.VMEM((3 * group, model), BF16),
            pltpu.VMEM((2 * group, model), BF16),
            pltpu.VMEM((NTILE * group, model), BF16),
            pltpu.VMEM((tokens, group), BF16),
            pltpu.VMEM((tokens + TXT_PAD, group), BF16),
            pltpu.VMEM((tokens + TXT_PAD, group), BF16),
            pltpu.VMEM((NTILE, 8, tokens + TXT_PAD), F32),
            pltpu.VMEM((NTILE, rows, group), BF16),
            pltpu.VMEM((NTILE, rows, group), BF16),
            pltpu.VMEM((rows, model), BF16),
            pltpu.VMEM((height + 2, LATC, width), BF16),
            pltpu.VMEM((9 * LATC, height * width), BF16),
            dma((2, NTILE)),
            dma((NTILE,)),
            dma((NTILE,)),
            dma((NTILE,)),
            dma((6, 4)),
            dma((6,)),
            dma((4, 4)),
            dma((4,)),
            dma((7,)),
            dma((8,)),
            dma((NTILE,)),
            dma((NTILE,)),
            dma((2,)),
            dma((2,)),
            dma((11,)),
        ],
        compiler_params=pltpu.CompilerParams(
            collective_id=0, has_side_effects=True, vmem_limit_bytes=48 * 1024 * 1024
        ),
        name="split_heads",
    )(
        x_img[0], x_txt[0], modulation.transpose(1, 0, 2), w_img.T, w_txt.T, w_out, w_final.T, bias,
        jnp.full((8, width), sigma_step, F32), latent[0],
    )
    features = jnp.dot(conv_w, stacked, preferred_element_type=F32).astype(BF16)
    return velocity[None], latent_next[None], features.reshape(1, -1, height, width)


def solution(mesh):
    fits = mesh.shape["blk"] == NTILE and mesh.shape["req"] == NREQ
    return jax.shard_map(
        split_heads if fits else on_device,
        mesh=mesh,
        in_specs=(
            P("req", "blk", None),
            P("req", None, None),
            P("req", None, None),
            P(None, "req"),
            P(None, "req"),
            P("req", None),
            P(),
            P("req"),
            P("req", "blk", None),
            P("req"),
            P("req", None, "blk", None),
            P(),
        ),
        out_specs=(
            P("req", None, "blk", None),
            P("req", None, "blk", None),
            P("req", None, "blk", None),
        ),
        check_vma=False,
    )
```

```python
import jax
import jax.numpy as jnp
from jax import lax
from jax.experimental import pallas as pl
from jax.experimental.pallas import tpu as pltpu
from jax.sharding import PartitionSpec as P

HD = 64
GRIDW = 64
PATCH = 2
LATC = 16
NSTEPS = 28


NORM_EPS = 1e-06
SHIFT_FACTOR = 3.0
LATENT_SCALE = 1.5305
LATENT_SHIFT = 0.0609
NEG_LARGE = -1e30
SCORE_SCALE = 0.125


def with_halo(block, sides, width):
    for axis, dim in sides:
        count = lax.axis_size(axis)
        forward = [(i, i + 1) for i in range(count - 1)]
        backward = [(target, source) for source, target in forward]
        low = lax.ppermute(
            lax.slice_in_dim(block, block.shape[dim] - width, None, axis=dim), axis, forward
        )
        high = lax.ppermute(lax.slice_in_dim(block, 0, width, axis=dim), axis, backward)
        block = jnp.concatenate([low, block, high], axis=dim)
    return block


def layer_norm(values):
    values = values.astype(jnp.float32)
    center = values - jnp.mean(values, axis=-1, keepdims=True)
    spread = jnp.mean(center * center, axis=-1, keepdims=True)
    return center * lax.rsqrt(spread + NORM_EPS)


def modulate(values, shift_row, scale_row):
    return layer_norm(values) * (1.0 + scale_row) + shift_row


def sigma_of(step_index, step_count):
    fraction = 1.0 - step_index.astype(jnp.float32) / step_count
    return SHIFT_FACTOR * fraction / (1.0 + (SHIFT_FACTOR - 1.0) * fraction)


def unpatchify(token_out, grid_width, patch_size, channels):
    patch_rows = token_out.shape[0] // grid_width
    shaped = token_out.reshape(patch_rows, grid_width, patch_size, patch_size, channels)
    shaped = jnp.transpose(shaped, (4, 0, 2, 1, 3))
    return shaped.reshape(channels, patch_rows * patch_size, grid_width * patch_size)


def convolve(padded, conv_w):
    row_count = padded.shape[1] - 2
    col_count = padded.shape[2] - 2
    tap_list = [
        padded[:, tap_row : tap_row + row_count, tap_col : tap_col + col_count]
        for tap_row in range(3)
        for tap_col in range(3)
    ]
    stacked = jnp.stack(tap_list, axis=1).reshape(padded.shape[0] * 9, row_count * col_count)
    convolved = jnp.dot(conv_w, stacked, preferred_element_type=jnp.float32)
    return convolved.reshape(conv_w.shape[0], row_count, col_count)


def text_state(queries, keys_txt, vals_txt, length):
    text_allowed = (jnp.arange(keys_txt.shape[0], dtype=jnp.int32) < length)[None, None, :]
    text_scores = (
        jnp.einsum("qhd,khd->qhk", queries, keys_txt, preferred_element_type=jnp.float32)
        * SCORE_SCALE
    )
    text_scores = jnp.where(text_allowed, text_scores, NEG_LARGE)
    text_max = jnp.max(text_scores, axis=2)
    text_weights = jnp.where(text_allowed, jnp.exp(text_scores - text_max[:, :, None]), 0.0)
    text_acc = jnp.einsum(
        "qhk,khd->qhd",
        text_weights.astype(jnp.bfloat16),
        vals_txt,
        preferred_element_type=jnp.float32,
    )
    return (text_max, jnp.sum(text_weights, axis=2), text_acc)


def absorb_block(previous, queries, head_keys, head_vals, allowed):
    old_max, old_sum, old_acc = previous
    scores = (
        jnp.einsum("qhd,khd->qhk", queries, head_keys, preferred_element_type=jnp.float32)
        * SCORE_SCALE
    )
    scores = jnp.where(allowed, scores, NEG_LARGE)
    new_max = jnp.maximum(old_max, jnp.max(scores, axis=2))
    weights = jnp.where(allowed, jnp.exp(scores - new_max[:, :, None]), 0.0)
    factor = jnp.exp(old_max - new_max)
    summed = jnp.einsum(
        "qhk,khd->qhd", weights.astype(jnp.bfloat16), head_vals, preferred_element_type=jnp.float32
    )
    return (
        new_max,
        old_sum * factor + jnp.sum(weights, axis=2),
        old_acc * factor[:, :, None] + summed,
    )


def absorb_maybe(previous, queries, head_keys, head_vals, allowed):
    return absorb_block(previous, queries, head_keys, head_vals, allowed)


def on_device(
    x_img,
    x_txt,
    modulation,
    w_img,
    w_txt,
    w_out,
    w_final,
    lengths,
    block_mask,
    timestep,
    latent,
    conv_w,
):
    tokens = x_img[0]
    factors = modulation[0]
    tok_rows = tokens.shape[0]
    head_cols = w_out.shape[0] * lax.axis_size("req")
    head_count = head_cols // HD
    h_img = modulate(tokens, factors[0], factors[1]).astype(jnp.bfloat16)
    h_txt = modulate(x_txt[0], factors[3], factors[4]).astype(jnp.bfloat16)
    qkv = jnp.dot(
        h_img, lax.all_gather(w_img, "req", axis=1, tiled=True), preferred_element_type=jnp.float32
    ).astype(jnp.bfloat16)
    kv_txt = jnp.dot(
        h_txt, lax.all_gather(w_txt, "req", axis=1, tiled=True), preferred_element_type=jnp.float32
    ).astype(jnp.bfloat16)
    keys_txt = kv_txt[:, :head_cols].reshape(-1, head_count, HD)
    vals_txt = kv_txt[:, head_cols:].reshape(-1, head_count, HD)
    length = lengths[0]
    queries = qkv[:, :head_cols].reshape(tok_rows, head_count, HD)
    keys_img = qkv[:, head_cols : 2 * head_cols]
    vals_img = qkv[:, 2 * head_cols :]
    mask_row = block_mask[0, 0]
    tile_count = mask_row.shape[0]
    start_state = text_state(queries, keys_txt, vals_txt, length)
    piece_keys = lax.all_gather(keys_img, "blk", axis=0, tiled=True)
    piece_vals = lax.all_gather(vals_img, "blk", axis=0, tiled=True)
    piece_len = piece_keys.shape[0]
    key_tile = jnp.arange(piece_len, dtype=jnp.int32) // tok_rows
    tile_hit = key_tile[:, None] == jnp.arange(tile_count, dtype=jnp.int32)[None, :]
    allowed = jnp.sum(jnp.where(tile_hit, mask_row[None, :], 0), axis=1) == 1
    head_keys = piece_keys.reshape(piece_len, head_count, HD)
    head_vals = piece_vals.reshape(piece_len, head_count, HD)
    run_max, run_sum, run_acc = absorb_maybe(
        start_state, queries, head_keys, head_vals, allowed[None, None, :]
    )
    attended = (run_acc / run_sum[:, :, None]).reshape(tok_rows, head_cols).astype(jnp.bfloat16)
    projected = jnp.dot(
        attended,
        lax.all_gather(w_out, "req", axis=0, tiled=True),
        preferred_element_type=jnp.float32,
    )
    residual = tokens.astype(jnp.float32) + factors[2] * projected
    final_in = modulate(residual, factors[5], factors[6]).astype(jnp.bfloat16)
    token_out = jnp.dot(final_in, w_final, preferred_element_type=jnp.float32)
    velocity = unpatchify(token_out, GRIDW, PATCH, LATC)[None]
    step_index = timestep[0]
    sigma_step = sigma_of(step_index + 1, NSTEPS) - sigma_of(step_index, NSTEPS)
    latent_next = latent + sigma_step * velocity
    decoded = (latent_next / LATENT_SCALE + LATENT_SHIFT).astype(jnp.bfloat16)
    padded = with_halo(decoded, (("blk", 2),), 1)
    padded = jnp.pad(padded[0], ((0, 0), (0, 0), (1, 1)))
    features = convolve(padded, conv_w).astype(jnp.bfloat16)[None]
    return (velocity, latent_next, features)


MESH = pl.DeviceIdType.MESH
NTILE = 4
NREQ = 8
CHUNK = 96
TXT_PAD = 256
F32 = jnp.float32
BF16 = jnp.bfloat16


def nt_dot(a, b):
    return lax.dot_general(a, b, (((1,), (1,)), ((), ())), preferred_element_type=F32)


def flip(r, bit):
    return r + bit - 2 * bit * ((r // bit) % 2)


def normed(v):
    v = v.astype(F32)
    c = v - jnp.mean(v, axis=-1, keepdims=True)
    return c * lax.rsqrt(jnp.mean(c * c, axis=-1, keepdims=True) + NORM_EPS)


def kernel(
    x_ref, xt_ref, mod_ref, wi_ref, wt_ref, wo_ref, wf_ref, bias_ref, ss_ref, lat_ref,
    vel_ref, next_ref, stk_ref,
    H, HT, WI, WT, WO, Q, K, V, BIAS, A, AT, FIN, DEC, STK,
    z_send, h_recv, b_send, b_recv, wi_send, wi_recv, wt_send, wt_recv,
    wo_send, wo_recv, a_send, a_recv, d_send, d_recv, l_sem,
):
    r = lax.axis_index("req")
    z = lax.axis_index("blk")
    rows = x_ref.shape[0]
    tokens = rows * NTILE
    group = WI.shape[0] // 3
    sib = flip(r, 1)
    nx = flip(r, 2)
    ny = flip(r, 4)
    nd = flip(nx, 4)

    def rcopy(src, dst, ss, rs, **dev):
        return pltpu.make_async_remote_copy(
            src_ref=src, dst_ref=dst, send_sem=ss, recv_sem=rs, device_id=dev, device_id_type=MESH
        )

    barrier = pltpu.get_barrier_semaphore()
    for step in range(1, NREQ):
        pl.semaphore_signal(
            barrier, inc=1, device_id={"req": lax.rem(r + step, NREQ)}, device_id_type=MESH
        )
    for step in range(1, NTILE):
        pl.semaphore_signal(
            barrier, inc=1, device_id={"blk": lax.rem(z + step, NTILE)}, device_id_type=MESH
        )
    def norm_rows(i, src, dst, shift, scale):
        at = pl.ds(pl.multiple_of(i * 32, 32), 32)
        dst[at, :] = (normed(src[at, :]) * (1.0 + mod_ref[scale]) + mod_ref[shift]).astype(BF16)

    own = H.at[z]
    pl.loop(0, rows // 32)(lambda i: norm_rows(i, x_ref, own, 0, 1))

    pl.semaphore_wait(barrier, NREQ - 1 + NTILE - 1)

    pieces = []
    for j in range(6):
        via = j % 2
        cid = 8 * (j // 2) + 2 * z + j % 2
        off = pl.multiple_of((cid % 3) * CHUNK, CHUNK)
        pieces.append(
            (wi_ref.at[pl.ds(off, CHUNK)], WI.at[pl.ds(j * CHUNK, CHUNK)], cid // 3, via, wi_send.at[j], wi_recv.at[j], l_sem.at[j])
        )
    for j in range(4):
        part = pl.ds((j % 2) * CHUNK, CHUNK)
        pieces.append(
            (wt_ref.at[part], WT.at[pl.ds(j * CHUNK, CHUNK)], 4 * (j // 2) + z, j % 2, wt_send.at[j], wt_recv.at[j], l_sem.at[6 + j])
        )

    def up(t):
        return rcopy(H.at[t], H.at[t], z_send.at[0, t], h_recv.at[t], blk=z + 1)

    def down(t):
        return rcopy(H.at[t], H.at[t], z_send.at[1, t], h_recv.at[t], blk=z - 1)

    @pl.when(z < NTILE - 1)
    def _():
        up(z).start()

    @pl.when(z > 0)
    def _():
        down(z).start()

    for src, slot, owner, via, ss, rs, ls in pieces:
        @pl.when(owner == r)
        def _():
            for n, dev in enumerate((nx, ny, sib)):
                rcopy(src, slot, ss.at[n], rs, req=dev).start()
            pltpu.make_async_copy(src, slot, ls).start()

    def take(step):
        low, high = z - step, z + step

        @pl.when(low >= 0)
        def _():
            rcopy(H.at[low], H.at[low], z_send.at[0, low], h_recv.at[low], blk=z).wait_recv()

            @pl.when(z < NTILE - 1)
            def _():
                up(low).start()

        @pl.when(high < NTILE)
        def _():
            rcopy(H.at[high], H.at[high], z_send.at[1, high], h_recv.at[high], blk=z).wait_recv()

            @pl.when(z > 0)
            def _():
                down(high).start()

    BIAS[z] = bias_ref[...]
    for step in range(1, NTILE):
        rcopy(BIAS.at[z], BIAS.at[z], b_send.at[step], b_recv.at[NTILE - step], blk=lax.rem(z + step, NTILE)).start()

    whole = xt_ref.shape[0] // 32 * 32
    pl.loop(0, whole // 32)(lambda i: norm_rows(i, xt_ref, HT, 3, 4))
    rest = (normed(xt_ref[whole:, :]) * (1.0 + mod_ref[4]) + mod_ref[3]).astype(BF16)
    filler = jnp.zeros((TXT_PAD - xt_ref.shape[0], rest.shape[1]), BF16)
    HT[whole:, :] = jnp.concatenate([rest, filler], axis=0)

    for src, slot, owner, via, ss, rs, ls in pieces:
        near, onward = ((nx, ny), (ny, nx))[via]

        @pl.when(jnp.logical_or(owner == nx, owner == ny))
        def _():
            rcopy(src, slot, ss.at[0], rs, req=sib).wait_recv()
            rcopy(slot, slot, ss.at[0], rs, req=sib).start()

        @pl.when(owner == near)
        def _():
            rcopy(slot, slot, ss.at[1], rs, req=onward).start()

    take(1)

    for src, slot, owner, via, ss, rs, ls in pieces:
        @pl.when(owner == r)
        def _():
            pltpu.make_async_copy(src, slot, ls).wait()

        @pl.when(owner == nd)
        def _():
            rcopy(src, slot, ss.at[0], rs, req=sib).wait_recv()
            rcopy(slot, slot, ss.at[0], rs, req=sib).start()

        @pl.when(owner % 2 != r % 2)
        def _():
            rcopy(src, slot, ss.at[0], rs, req=sib).wait_recv()

    def wo_rows(dev):
        return WO.at[pl.ds(pl.multiple_of(dev * CHUNK, CHUNK), CHUNK)]

    for n, (k, dev) in enumerate(((2, nx), (4, ny), (6, nd), (1, sib))):
        rcopy(wo_ref, wo_rows(r), wo_send.at[n], wo_recv.at[k], req=dev).start()
    pltpu.make_async_copy(wo_ref, wo_rows(r), l_sem.at[10]).start()

    kv = nt_dot(HT[...], WT[...]).astype(BF16)
    K[tokens:, :] = kv[:, :group]
    V[tokens:, :] = kv[:, group:]

    def project(t):
        at = pl.ds(pl.multiple_of(t * rows, rows), rows)
        qkv = nt_dot(H[t], WI[...]).astype(BF16)
        Q[at, :] = qkv[:, :group] * jnp.asarray(SCORE_SCALE, BF16)
        K[at, :] = qkv[:, group : 2 * group]
        V[at, :] = qkv[:, 2 * group :]

    project(z)
    for step in range(1, NTILE):
        low, high = z - step, z + step
        if step > 1:
            take(step)
        if step == 2:
            for n, (k, dev) in enumerate(((2, nx), (4, ny), (6, nd))):
                rows_of = wo_rows(dev)
                rcopy(wo_ref, rows_of, wo_send.at[n], wo_recv.at[k], req=sib).wait_recv()
                rcopy(rows_of, rows_of, wo_send.at[4 + n], wo_recv.at[k + 1], req=sib).start()

        @pl.when(low >= 0)
        def _():
            project(low)

        @pl.when(high < NTILE)
        def _():
            project(high)

    for step in range(1, NTILE):
        src = BIAS.at[lax.rem(z + step, NTILE)]
        rcopy(src, src, b_send.at[step], b_recv.at[step], blk=lax.rem(z + step, NTILE)).wait_recv()

    def attend(t):
        at = pl.ds(pl.multiple_of(t * rows, rows), rows)
        bias = BIAS[t][0:1, :]
        q, k, v = Q[at, :], K[...], V[...]
        outs = []
        for h in range(group // HD):
            cols = slice(h * HD, (h + 1) * HD)
            s = nt_dot(q[:, cols], k[:, cols]) + bias
            p = jnp.exp(s - jnp.max(s, axis=1, keepdims=True))
            total = jnp.sum(p, axis=1, keepdims=True)
            o = jnp.dot(p.astype(BF16), v[:, cols], preferred_element_type=F32)
            outs.append(o / total)
        return jnp.concatenate(outs, axis=1).astype(BF16)

    for step in range(1, NTILE):
        t = lax.rem(z + step, NTILE)
        A[step] = attend(t)
        rcopy(A.at[step], AT.at[z], a_send.at[step], a_recv.at[NTILE - step], blk=t).start()
    AT[z] = attend(z)

    pltpu.make_async_copy(wo_ref, wo_rows(r), l_sem.at[10]).wait()
    rcopy(wo_ref, wo_rows(sib), wo_send.at[3], wo_recv.at[1], req=sib).wait_recv()
    for n, (k, dev) in enumerate(((3, nx), (5, ny), (7, nd))):
        rcopy(wo_ref, wo_rows(flip(dev, 1)), wo_send.at[4 + n], wo_recv.at[k], req=sib).wait_recv()
    for step in range(1, NTILE):
        src = AT.at[lax.rem(z + step, NTILE)]
        rcopy(src, src, a_send.at[step], a_recv.at[step], blk=lax.rem(z + step, NTILE)).wait_recv()

    def out_rows(i):
        at = pl.ds(pl.multiple_of(i * 64, 64), 64)
        proj = jnp.dot(AT[0, at, :], WO[0:group, :], preferred_element_type=F32)
        for s in range(1, NTILE):
            proj += jnp.dot(AT[s, at, :], WO[s * group : (s + 1) * group, :], preferred_element_type=F32)
        res = x_ref[at, :].astype(F32) + mod_ref[2] * proj
        FIN[at, :] = (normed(res) * (1.0 + mod_ref[6]) + mod_ref[5]).astype(BF16)

    pl.loop(0, rows // 64)(out_rows)

    dup = (
        lax.broadcasted_iota(jnp.int32, (2 * rows, rows), 0) // 2
        == lax.broadcasted_iota(jnp.int32, (2 * rows, rows), 1)
    ).astype(F32).astype(BF16)
    twice = jnp.dot(dup, FIN[...], preferred_element_type=F32).astype(BF16)
    tok = nt_dot(wf_ref[...], twice)
    even = lax.broadcasted_iota(jnp.int32, (LATC, 2 * rows), 1) % 2 == 0
    width = PATCH * GRIDW
    sig = ss_ref[0:1, :]
    for p in range(PATCH):
        base = p * 2 * LATC
        val = jnp.where(even, tok[base : base + LATC], tok[base + LATC : base + 2 * LATC])
        for a in range(rows // GRIDW):
            y = PATCH * a + p
            piece = val[:, a * width : (a + 1) * width]
            nxt = lat_ref[:, y, :] + sig * piece
            vel_ref[:, y, :] = piece
            next_ref[:, y, :] = nxt
            DEC[y + 1] = (nxt / LATENT_SCALE + LATENT_SHIFT).astype(BF16)

    count = PATCH * rows // GRIDW
    go_up = rcopy(DEC.at[count], DEC.at[0], d_send.at[0], d_recv.at[0], blk=z + 1)
    go_down = rcopy(DEC.at[1], DEC.at[count + 1], d_send.at[1], d_recv.at[1], blk=z - 1)

    @pl.when(z < NTILE - 1)
    def _():
        go_up.start()

    @pl.when(z > 0)
    def _():
        go_down.start()

    @pl.when(z == 0)
    def _():
        DEC[0] = jnp.zeros((LATC, width), BF16)

    @pl.when(z == NTILE - 1)
    def _():
        DEC[count + 1] = jnp.zeros((LATC, width), BF16)

    for src, slot, owner, via, ss, rs, ls in pieces:
        near = (nx, ny)[via]

        @pl.when(owner == r)
        def _():
            for n in range(3):
                rcopy(src, slot, ss.at[n], rs, req=sib).wait_send()

        @pl.when(jnp.logical_and(owner != r, owner % 2 == r % 2))
        def _():
            rcopy(slot, slot, ss.at[0], rs, req=sib).wait_send()

        @pl.when(owner == near)
        def _():
            rcopy(slot, slot, ss.at[1], rs, req=sib).wait_send()

    for n in range(7):
        rcopy(wo_ref, wo_rows(r), wo_send.at[n], wo_recv.at[1], req=sib).wait_send()
    for t in range(NTILE):
        @pl.when(jnp.logical_and(z < NTILE - 1, t <= z))
        def _():
            up(t).wait_send()

        @pl.when(jnp.logical_and(z > 0, t >= z))
        def _():
            down(t).wait_send()
    for step in range(1, NTILE):
        there = lax.rem(z + step, NTILE)
        rcopy(BIAS.at[z], BIAS.at[z], b_send.at[step], b_recv.at[step], blk=there).wait_send()
        rcopy(A.at[step], AT.at[z], a_send.at[step], a_recv.at[step], blk=there).wait_send()

    @pl.when(z < NTILE - 1)
    def _():
        go_up.wait_send()
        go_down.wait_recv()

    @pl.when(z > 0)
    def _():
        go_down.wait_send()
        go_up.wait_recv()

    lane = lax.broadcasted_iota(jnp.int32, (LATC, width), 1)
    for yy in range(count + 2):
        mid = DEC[yy].astype(F32)
        shifted = (
            jnp.where(lane == 0, 0.0, pltpu.roll(mid, 1, 1)),
            mid,
            jnp.where(lane == width - 1, 0.0, pltpu.roll(mid, width - 1, 1)),
        )
        for a in range(3):
            y = yy - a
            if 0 <= y < count:
                for b in range(3):
                    at = (3 * a + b) * LATC
                    STK[at : at + LATC, y * width : (y + 1) * width] = shifted[b].astype(BF16)

    taps = 9 * LATC
    row = lax.broadcasted_iota(jnp.int32, (taps, taps), 0)
    col = lax.broadcasted_iota(jnp.int32, (taps, taps), 1)
    order = (row == (col % LATC) * 9 + col // LATC).astype(F32).astype(BF16)
    stk_ref[...] = jnp.dot(order, STK[...], preferred_element_type=F32).astype(BF16)


def split_heads(
    x_img, x_txt, modulation, w_img, w_txt, w_out, w_final, lengths, block_mask, timestep, latent, conv_w
):
    rows, model = x_img.shape[1], x_img.shape[2]
    group = w_out.shape[0] * NREQ // NTILE
    tokens = rows * NTILE
    allowed = jnp.concatenate(
        [jnp.repeat(block_mask[0, 0] == 1, rows), jnp.arange(TXT_PAD, dtype=jnp.int32) < lengths[0]]
    )
    bias = jnp.broadcast_to(jnp.where(allowed, 0.0, NEG_LARGE).astype(F32)[None, :], (8, tokens + TXT_PAD))
    step_index = timestep[0]
    sigma_step = sigma_of(step_index + 1, NSTEPS) - sigma_of(step_index, NSTEPS)
    height, width = latent.shape[2], latent.shape[3]
    vmem = pl.BlockSpec(memory_space=pltpu.VMEM)
    hbm = pl.BlockSpec(memory_space=pl.ANY)
    dma = pltpu.SemaphoreType.DMA
    velocity, latent_next, stacked = pl.pallas_call(
        kernel,
        out_shape=(
            jax.ShapeDtypeStruct((LATC, height, width), F32),
            jax.ShapeDtypeStruct((LATC, height, width), F32),
            jax.ShapeDtypeStruct((9 * LATC, height * width), BF16),
        ),
        in_specs=[vmem, vmem, vmem, hbm, hbm, hbm, vmem, vmem, vmem, vmem],
        out_specs=(vmem, vmem, vmem),
        scratch_shapes=[
            pltpu.VMEM((NTILE, rows, model), BF16),
            pltpu.VMEM((TXT_PAD, model), BF16),
            pltpu.VMEM((3 * group, model), BF16),
            pltpu.VMEM((2 * group, model), BF16),
            pltpu.VMEM((NTILE * group, model), BF16),
            pltpu.VMEM((tokens, group), BF16),
            pltpu.VMEM((tokens + TXT_PAD, group), BF16),
            pltpu.VMEM((tokens + TXT_PAD, group), BF16),
            pltpu.VMEM((NTILE, 8, tokens + TXT_PAD), F32),
            pltpu.VMEM((NTILE, rows, group), BF16),
            pltpu.VMEM((NTILE, rows, group), BF16),
            pltpu.VMEM((rows, model), BF16),
            pltpu.VMEM((height + 2, LATC, width), BF16),
            pltpu.VMEM((9 * LATC, height * width), BF16),
            dma((2, NTILE)),
            dma((NTILE,)),
            dma((NTILE,)),
            dma((NTILE,)),
            dma((6, 4)),
            dma((6,)),
            dma((4, 4)),
            dma((4,)),
            dma((7,)),
            dma((8,)),
            dma((NTILE,)),
            dma((NTILE,)),
            dma((2,)),
            dma((2,)),
            dma((11,)),
        ],
        compiler_params=pltpu.CompilerParams(
            collective_id=0, has_side_effects=True, vmem_limit_bytes=60 * 1024 * 1024
        ),
        name="split_heads",
    )(
        x_img[0], x_txt[0], modulation.transpose(1, 0, 2), w_img.T, w_txt.T, w_out, w_final.T, bias,
        jnp.full((8, width), sigma_step, F32), latent[0],
    )
    features = jnp.dot(conv_w, stacked, preferred_element_type=F32).astype(BF16)
    return velocity[None], latent_next[None], features.reshape(1, -1, height, width)


def solution(mesh):
    fits = mesh.shape["blk"] == NTILE and mesh.shape["req"] == NREQ
    return jax.shard_map(
        split_heads if fits else on_device,
        mesh=mesh,
        in_specs=(
            P("req", "blk", None),
            P("req", None, None),
            P("req", None, None),
            P(None, "req"),
            P(None, "req"),
            P("req", None),
            P(),
            P("req"),
            P("req", "blk", None),
            P("req"),
            P("req", None, "blk", None),
            P(),
        ),
        out_specs=(
            P("req", None, "blk", None),
            P("req", None, "blk", None),
            P("req", None, "blk", None),
        ),
        check_vma=False,
    )
```
